32 devices in a mesh: dp: 2 (over x), ctx: 16 (over z, y, core).
Axes of the slice: x: 2, y: 2, z: 4, core: 2. Of those that a mesh axis runs over, the one named last changes fastest.
Arguments:
- layer_input: bfloat16 [2, 2048, 8192], P('dp', 'ctx'), may hold values from -6 to 6
- queries: bfloat16 [2, 2048, 1024], P('dp', 'ctx'), may hold values from -6 to 6
- keys: bfloat16 [2, 2048, 128], P('dp', 'ctx'), may hold values from -6 to 6
- values: bfloat16 [2, 2048, 128], P('dp', 'ctx'), may hold values from -6 to 6
- d_out: bfloat16 [2, 2048, 1024], P('dp', 'ctx'), may hold values from -6 to 6
- doc_lengths: int32 [2, 8], P('dp'), may hold values from 1 to 512, 2048 in all within a row
- block_order: int32 [32], replicated, may hold values from 0 to 31, as said below
Outputs:
- query_grad: bfloat16 [2, 2048, 1024], P('dp', 'ctx')
- key_grad: bfloat16 [2, 2048, 128], P('dp', 'ctx')
- value_grad: bfloat16 [2, 2048, 128], P('dp', 'ctx')
- kv_weight_grad: float32 [16, 512, 256], P('ctx', 'dp')
The draws below stay inside these ranges and needn't reach their ends.
Inputs may be any that keep to these rules, and one draw needn't show every extreme that they name: `block_order`: entries 2r and 2r+1 are the blocks stored in rows 2r*64 to 2r*64 + 2*64 - 1; they sum to 31, and every block appears once.
All inputs are finite; a program needn't handle non-finite values.
Results may differ from the reference program's by a relative error of at most 0.012.
Values may be sent and summed in bfloat16 or wider, within the bound.
No kernel may reach another device: no remote copies, remote signals or barrier semaphores. Data moves between devices by JAX's collectives and lax.ppermute only.
A program may use at most 64 MiB of HBM per device.

```python
import math
import jax
import jax.numpy as jnp
import numpy as np
from jax import lax

D = 8192
HD = 128
HEADS = 8
NDOCS = 8
HALF = 64
BLOCKS = 32
SEQ = 2048
SEQS = 2
N_CTX = 16


def draw_queries(key, part):
    first = jax.random.fold_in(jax.random.fold_in(key, 1), 0)
    result = jnp.clip(jax.random.normal(first, (SEQS, SEQ, HEADS, HD), jnp.float32), -6.0, 6.0)
    return result.reshape(SEQS, SEQ, HEADS * HD).astype(jnp.bfloat16)


def draw_keys(key, part):
    first = jax.random.fold_in(jax.random.fold_in(key, 2), 0)
    result = jnp.clip(jax.random.normal(first, (SEQS, SEQ, HD), jnp.float32), -6.0, 6.0)
    return result.astype(jnp.bfloat16)


def draw_block_order(key, part):
    first, second = jax.random.split(jax.random.fold_in(key, 3))
    count = BLOCKS // 2
    chosen = jax.random.permutation(first, count).astype(jnp.int32)
    flips = jax.random.randint(second, (count,), 0, 2)
    lower = jnp.where(flips == 1, BLOCKS - 1 - chosen, chosen).astype(jnp.int32)
    return jnp.stack([lower, BLOCKS - 1 - lower], axis=1).reshape(BLOCKS).astype(jnp.int32)


def block_levels(key, shape, cuts, least, largest):
    loudness = 1.0
    for position, blocks in cuts:
        draws = jax.random.uniform(jax.random.fold_in(jax.random.fold_in(key, 6), position), (blocks,), jnp.float32, least / len(cuts), largest / len(cuts))
        loudness = loudness * jnp.repeat(jnp.exp(draws), shape[position] // blocks).reshape((-1,) + (1,) * (len(shape) - 1 - position))
    return loudness


def length_profile(number_of, total, limit, slope):
    loads = [(1 << 20) // math.isqrt(standing ** slope) + 1 for standing in range(2, number_of + 1)]
    rest, given = total - limit - (number_of - 1), [1] * (number_of - 1)
    while rest > 0:
        candidates = [i for i in range(number_of - 1) if given[i] < limit]
        whole, remaining = sum([loads[i] for i in candidates]), rest
        for i in candidates:
            addition = min(limit - given[i], max(1, remaining * loads[i] // whole), rest)
            given[i] = given[i] + addition
            rest = rest - addition
    return np.array([limit] + given)


def uneven_parts(stream_key, amount, total, most, lean):
    if amount == 2:
        one = jax.random.randint(stream_key, (), max(1, total - most), min(most, total - 1) + 1)
        return jnp.stack([one, total - one])
    tallies = jnp.asarray(length_profile(amount, total, most, lean), jnp.int32)
    couples = (amount - 1) // 2
    giver, receiver = tallies[1:1 + 2 * couples:2], tallies[2:2 + 2 * couples:2]
    margin = jnp.minimum(giver - 1, most - receiver)
    passed = jax.random.randint(jax.random.fold_in(stream_key, 1), (couples,), 0, 1 << 20) % (margin + 1)
    tallies = tallies.at[1:1 + 2 * couples:2].set(giver - passed).at[2:2 + 2 * couples:2].set(receiver + passed)
    return tallies[jax.random.permutation(jax.random.fold_in(stream_key, 2), amount)]


def normal_values(rng, shape, deviation, most, cuts=(), kind=jnp.bfloat16):
    entries = deviation * jax.random.normal(rng, shape, jnp.float32)
    if cuts:
        entries = entries * block_levels(rng, shape, cuts, -0.22, 0.18)
    return jnp.clip(entries, -most, most).astype(kind)


def setup_inputs(seed: int = 0) -> dict:
    key_of = jax.random.split(jax.random.key(seed), 8)
    layer_input = normal_values(key_of[0], (SEQS, SEQ, D), 1.0, 6.0, ((0, 2), (1, 16)))
    queries = draw_queries(jax.random.fold_in(key_of[7], 71), 0)
    keys = draw_keys(jax.random.fold_in(key_of[7], 71), 0)
    values = normal_values(key_of[3], (SEQS, SEQ, HD), 1.0, 6.0, ((0, 2), (1, 16)))
    d_out = normal_values(key_of[4], (SEQS, SEQ, HEADS * HD), 1.0, 6.0, ((0, 2), (1, 16)))
    doc_lengths = jax.vmap(lambda own: uneven_parts(own, NDOCS, SEQ, SEQ // 4, 2))(jax.random.split(key_of[5], SEQS)).reshape((SEQS, NDOCS)).astype(jnp.int32)
    block_order = draw_block_order(jax.random.fold_in(key_of[7], 71), 0)
    return {"layer_input": layer_input, "queries": queries, "keys": keys, "values": values, "d_out": d_out, "doc_lengths": doc_lengths, "block_order": block_order}


def reference(layer_input, queries, keys, values, d_out, doc_lengths, block_order):
    scale = 1.0 / math.sqrt(HD)
    qblock = 512
    nblk = SEQ // qblock
    key_pos = (block_order[:, None] * HALF + jnp.arange(HALF, dtype=jnp.int32)[None, :]).reshape(SEQ).astype(jnp.int32)
    q_list = []
    k_list = []
    v_list = []
    weight = jnp.zeros((D, 2 * HD), jnp.float32)
    for seq in range(SEQS):
        ends = jnp.cumsum(doc_lengths[seq]).astype(jnp.int32)
        key_doc = lax.optimization_barrier(jnp.sum((key_pos[:, None] >= ends[None, :]).astype(jnp.int32), axis=1)).astype(jnp.int32)
        kfull = keys[seq].astype(jnp.float32)
        vfull = values[seq].astype(jnp.float32)
        qrows = queries[seq].astype(jnp.float32).reshape(nblk, qblock, HEADS, HD)
        drows = d_out[seq].astype(jnp.float32).reshape(nblk, qblock, HEADS, HD)
        qpos = key_pos.reshape(nblk, qblock)
        qdoc = key_doc.reshape(nblk, qblock)

        def step(carry, item):
            dk_sum, dv_sum = carry
            qb, db, pq, dq_doc = item
            mask = ((key_pos[None, :] <= pq[:, None]) & (key_doc[None, :] == dq_doc[:, None]))[None]
            s = jnp.einsum('thd,kd->htk', qb, kfull) * scale
            top = lax.optimization_barrier(jnp.max(jnp.where(mask, s, -1e+30), axis=2))
            total = lax.optimization_barrier(jnp.sum(jnp.where(mask, jnp.exp(s - top[..., None]), 0.0), axis=2))
            lse = top + jnp.log(total)
            p = jnp.where(mask, jnp.exp(s - lse[..., None]), 0.0)
            pb = lax.optimization_barrier(p.astype(jnp.bfloat16)).astype(jnp.float32)
            dprob = jnp.einsum('thd,kd->htk', db, vfull)
            delta = lax.optimization_barrier(jnp.sum(p * dprob, axis=2))
            ds = lax.optimization_barrier((p * (dprob - delta[..., None])).astype(jnp.bfloat16)).astype(jnp.float32)
            dq = (jnp.einsum('htk,kd->thd', ds, kfull) * scale).astype(jnp.bfloat16).reshape(qblock, HEADS * HD)
            dk_sum = dk_sum + jnp.einsum('htk,thd->kd', ds, qb)
            dv_sum = dv_sum + jnp.einsum('htk,thd->kd', pb, db)
            return ((dk_sum, dv_sum), dq)
        init = (jnp.zeros((SEQ, HD), jnp.float32), jnp.zeros((SEQ, HD), jnp.float32))
        (dk_sum, dv_sum), dq_blocks = lax.scan(step, init, (qrows, drows, qpos, qdoc))
        key_full = dk_sum * scale
        q_list.append(dq_blocks.reshape(SEQ, HEADS * HD))
        k_list.append(key_full.astype(jnp.bfloat16))
        v_list.append(dv_sum.astype(jnp.bfloat16))
        both = jnp.concatenate([key_full, dv_sum], axis=1)
        weight = weight + jnp.dot(layer_input[seq].astype(jnp.float32).T, both, preferred_element_type=jnp.float32, precision=lax.Precision.HIGHEST)
    weight = weight * (1.0 / math.sqrt(SEQS * SEQ))
    return (jnp.stack(q_list), jnp.stack(k_list), jnp.stack(v_list), weight.reshape(N_CTX, D // N_CTX, 2 * HD))
```

```python
import functools
import math

import jax
import jax.numpy as jnp
from jax import lax
from jax.experimental import pallas as pl
from jax.experimental.pallas import tpu as pltpu
from jax.sharding import PartitionSpec as P

NEG = -1e30
NT = (((1,), (1,)), ((), ()))
TN = (((0,), (0,)), ((), ()))


def attention_kernel(
    order, lengths, q_ref, d_ref, *refs, n, mid, top, heads, head_dim, half, blocks, window, group
):
    count = 2 * mid
    kv_refs = refs[:count]
    dq_ref = refs[count]
    out_refs = refs[count + 1 : 2 * count + 1]
    kv, kw, acc, inverse = refs[2 * count + 1 :]
    rank = lax.axis_index("ctx")
    rows = 2 * half
    share = top * rows
    for part in range(count):
        kv[part * share : (part + 1) * share, :] = kv_refs[part][...].reshape(share, 2 * head_dim)
    acc[...] = jnp.zeros_like(acc)

    def invert(i, carry):
        rel = jnp.bitwise_xor(i // 2, rank)
        core_rel = rel % 2
        mid_rel = (rel // 2) % mid
        top_rel = rel // (2 * mid)
        inverse[order[i]] = ((core_rel * mid + mid_rel) * top + top_rel) * rows + (i % 2) * half
        return carry

    lax.fori_loop(0, blocks, invert, 0)
    ends = []
    total = 0
    for k in range(lengths.shape[1]):
        total = total + lengths[0, k]
        ends.append(total)
    span = window * half
    scale = 1.0 / math.sqrt(head_dim)
    factor = scale * math.log2(math.e)
    lanes = group * half

    for t in range(2):
        block = order[2 * rank + t]
        first = jnp.clip(block - (window - 1), 0, blocks - window)
        for w in range(window):
            source = pl.multiple_of(inverse[first + w], half)
            kw[w * half : (w + 1) * half, :] = kv[pl.ds(source, half), :]
        k = kw[:, :head_dim]
        v = kw[:, head_dim:]
        kpos = first * half + lax.broadcasted_iota(jnp.int32, (span, lanes), 0)
        qpos = block * half + lax.broadcasted_iota(jnp.int32, (1, lanes), 1) % half
        start = jnp.zeros((1, lanes), jnp.int32)
        for end in ends:
            start = jnp.where(qpos >= end, end, start)
        mask = (kpos <= qpos) & (kpos >= start)
        dk = jnp.zeros((span, head_dim), jnp.float32)
        dv = jnp.zeros((span, head_dim), jnp.float32)
        trows = slice(t * half, (t + 1) * half)
        for g in range(heads // group):
            cols = [slice(h * head_dim, (h + 1) * head_dim) for h in range(g * group, (g + 1) * group)]
            q = jnp.concatenate([q_ref[trows, c] for c in cols], axis=0)
            d = jnp.concatenate([d_ref[trows, c] for c in cols], axis=0)
            s = lax.dot_general(k, q, NT, preferred_element_type=jnp.float32) * factor
            s = jnp.where(mask, s, NEG)
            e = jnp.exp2(s - jnp.max(s, axis=0, keepdims=True))
            inv = 1.0 / jnp.sum(e, axis=0, keepdims=True)
            p = e * inv
            dp = lax.dot_general(v, d, NT, preferred_element_type=jnp.float32)
            delta = jnp.sum(p * dp, axis=0, keepdims=True)
            ds = (p * (dp - delta)).astype(jnp.bfloat16)
            pb = p.astype(jnp.bfloat16)
            dv = dv + jnp.dot(pb, d, preferred_element_type=jnp.float32)
            dk = dk + jnp.dot(ds, q, preferred_element_type=jnp.float32)
            dq = lax.dot_general(k, ds, TN, preferred_element_type=jnp.float32) * scale
            dq = dq.T.astype(jnp.bfloat16)
            for i, c in enumerate(cols):
                dq_ref[trows, c] = dq[i * half : (i + 1) * half, :]
        dk = dk * scale
        for w in range(window):
            target = pl.ds(pl.multiple_of(inverse[first + w], half), half)
            acc[target, :head_dim] += dk[w * half : (w + 1) * half]
            acc[target, head_dim:] += dv[w * half : (w + 1) * half]
    for part in range(count):
        piece = acc[part * share : (part + 1) * share, :]
        out_refs[part][...] = piece.reshape(out_refs[part].shape).astype(out_refs[part].dtype)


def attention(order, lengths, q, d, kv_parts, *, n, mid, top):
    rows, width = q.shape
    head_dim = kv_parts[0].shape[2] // 2
    heads = width // head_dim
    half = rows // 2
    blocks = order.shape[0]
    window = min(blocks, 2 * ((blocks // 4 + 2) // 2))
    count = 2 * mid
    part = (top, rows, 2 * head_dim)
    body = functools.partial(
        attention_kernel,
        n=n,
        mid=mid,
        top=top,
        heads=heads,
        head_dim=head_dim,
        half=half,
        blocks=blocks,
        window=window,
        group=min(heads, 4),
    )
    vmem = pl.BlockSpec(memory_space=pltpu.VMEM)
    smem = pl.BlockSpec(memory_space=pltpu.SMEM)
    elements = 2 * heads * half * window * half
    return pl.pallas_call(
        body,
        out_shape=[jax.ShapeDtypeStruct((rows, width), jnp.bfloat16)]
        + [
            jax.ShapeDtypeStruct(part, jnp.float32 if i == 0 else jnp.bfloat16)
            for i in range(count)
        ],
        in_specs=[smem, smem, vmem, vmem] + [vmem] * count,
        out_specs=[vmem] * (count + 1),
        scratch_shapes=[
            pltpu.VMEM((n * rows, 2 * head_dim), jnp.bfloat16),
            pltpu.VMEM((window * half, 2 * head_dim), jnp.bfloat16),
            pltpu.VMEM((n * rows, 2 * head_dim), jnp.float32),
            pltpu.SMEM((blocks,), jnp.int32),
        ],
        cost_estimate=pl.CostEstimate(
            flops=10 * elements * head_dim, bytes_accessed=4 << 20, transcendentals=elements
        ),
        compiler_params=pltpu.CompilerParams(vmem_limit_bytes=40 << 20),
        name="attention_grads",
    )(order, lengths, q, d, *kv_parts)


def weight_kernel(x_ref, *refs, low):
    g_refs = refs[:low]
    out_refs = refs[low:-1]
    g_all = refs[-1]
    me = lax.axis_index("ctx") % low
    rows = g_refs[0].shape[0]
    for rel in range(low):
        place = pl.multiple_of(jnp.bitwise_xor(me, rel) * rows, rows)
        g_all[pl.ds(place, rows), :] = g_refs[rel][...]
    pieces = len(out_refs)
    height = x_ref.shape[1] // pieces
    for i in range(pieces):
        total = jnp.zeros((height, g_all.shape[1]), jnp.float32)
        for src in range(low):
            total = total + jnp.dot(
                x_ref[src, i * height : (i + 1) * height, :],
                g_all[src * rows : (src + 1) * rows, :],
                preferred_element_type=jnp.float32,
            )
        out_refs[i][...] = total.astype(out_refs[i].dtype)


def weight_terms(x, g_parts, pieces):
    low, height, rows = x.shape
    width = g_parts[0].shape[1]
    vmem = pl.BlockSpec(memory_space=pltpu.VMEM)
    shape = (height // pieces, width)
    return pl.pallas_call(
        functools.partial(weight_kernel, low=low),
        out_shape=[jax.ShapeDtypeStruct(shape, jnp.bfloat16)] * pieces,
        in_specs=[vmem] * (low + 1),
        out_specs=[vmem] * pieces,
        scratch_shapes=[pltpu.VMEM((low * rows, width), jnp.bfloat16)],
        cost_estimate=pl.CostEstimate(
            flops=2 * low * height * rows * width, bytes_accessed=4 << 20, transcendentals=0
        ),
        compiler_params=pltpu.CompilerParams(vmem_limit_bytes=24 << 20),
        name="weight_terms",
    )(x, *g_parts)


def per_device(layer_input, queries, keys, values, d_out, doc_lengths, block_order):
    n = lax.axis_size("ctx")
    dps = lax.axis_size("dp")
    rows = queries.shape[1]
    head_dim = keys.shape[2]
    width = layer_input.shape[2]
    top = 4
    mid = n // (2 * top)
    low = n // 2

    def swap(x, k):
        return lax.ppermute(x, "ctx", [(i, i ^ k) for i in range(n)])

    xt = layer_input[0].T.reshape(2, low, width // n, rows).transpose(1, 0, 2, 3)
    halves = [list(range(low)), list(range(low, n))]
    xt = lax.all_to_all(xt, "ctx", 0, 0, axis_index_groups=halves, tiled=True)
    xt = xt.reshape(low, 2 * (width // n), rows)

    kv = jnp.concatenate([keys[0], values[0]], axis=1)
    base = jnp.stack([kv] + [swap(kv, 2 * mid * j) for j in range(1, top)])
    near = [base] + [swap(base, 2 * j) for j in range(1, mid)]
    far = [swap(part, 1) for part in near]

    dq, *parts = attention(
        block_order, doc_lengths, queries[0], d_out[0], near + far, n=n, mid=mid, top=top
    )

    mine, others = parts[:mid], parts[mid:]
    received = [swap(p, 1) for p in reversed(others)][::-1]
    sends = [
        (mine[j].astype(jnp.float32) + received[j].astype(jnp.float32)).astype(jnp.bfloat16)
        for j in range(1, mid)
    ]
    total = mine[0].astype(jnp.float32) + received[0].astype(jnp.float32)
    for j in range(1, mid):
        total = total + swap(sends[j - 1], 2 * j).astype(jnp.float32)
    grad = total[0]
    for j in range(1, top):
        grad = grad + swap(total[j].astype(jnp.bfloat16), 2 * mid * j).astype(jnp.float32)
    grad16 = grad.astype(jnp.bfloat16)

    even = [grad16] + [swap(grad16, k) for k in range(2, low, 2)]
    gathered = [None] * low
    for i, g in enumerate(even):
        gathered[2 * i] = g
        gathered[2 * i + 1] = swap(g, 1)

    pieces = weight_terms(xt, gathered, 2 * dps)
    rank = lax.axis_index("ctx")
    side, mine_dp = rank // low, lax.axis_index("dp")
    pieces = jnp.stack(pieces).reshape(2, dps, width // n // dps, 2 * head_dim)
    weight = jnp.zeros(pieces.shape[2:], jnp.float32)
    for a in range(2):
        for b in range(dps):
            piece = lax.dynamic_slice(
                pieces, (side ^ a, mine_dp ^ b, 0, 0), (1, 1) + pieces.shape[2:]
            )[0, 0]
            if a or b:
                piece = lax.ppermute(
                    piece,
                    ("dp", "ctx"),
                    [(i * n + j, (i ^ b) * n + (j ^ (a * low))) for i in range(dps) for j in range(n)],
                )
            weight = weight + piece.astype(jnp.float32)
    weight = weight * (1.0 / math.sqrt(dps * rows * n))
    return (
        dq[None],
        grad16[None, :, :head_dim],
        grad16[None, :, head_dim:],
        weight[None],
    )


def solution(mesh):
    placed = (
        P("dp", "ctx", None),
        P("dp", "ctx", None),
        P("dp", "ctx", None),
        P("dp", "ctx", None),
        P("dp", "ctx", None),
        P("dp", None),
        P(),
    )
    return jax.shard_map(
        per_device,
        mesh=mesh,
        in_specs=placed,
        out_specs=(
            P("dp", "ctx", None),
            P("dp", "ctx", None),
            P("dp", "ctx", None),
            P("ctx", "dp", None),
        ),
        check_vma=False,
    )
```

```python
import functools
import math

import jax
import jax.numpy as jnp
from jax import lax
from jax.experimental import pallas as pl
from jax.experimental.pallas import tpu as pltpu
from jax.sharding import PartitionSpec as P

NEG = -1e30
NT = (((1,), (1,)), ((), ()))
TN = (((0,), (0,)), ((), ()))


def attention_kernel(
    order, lengths, q_ref, d_ref, *refs, n, mid, top, heads, head_dim, half, blocks, window, group
):
    count = 2 * mid
    kv_refs = refs[:count]
    dq_ref = refs[count]
    out_refs = refs[count + 1 : 2 * count + 1]
    kv, kw, acc, inverse = refs[2 * count + 1 :]
    rank = lax.axis_index("ctx")
    rows = 2 * half
    share = top * rows
    for part in range(count):
        kv[part * share : (part + 1) * share, :] = kv_refs[part][...].reshape(share, 2 * head_dim)
    acc[...] = jnp.zeros_like(acc)

    def invert(i, carry):
        rel = jnp.bitwise_xor(i // 2, rank)
        core_rel = rel % 2
        mid_rel = (rel // 2) % mid
        top_rel = rel // (2 * mid)
        inverse[order[i]] = ((core_rel * mid + mid_rel) * top + top_rel) * rows + (i % 2) * half
        return carry

    lax.fori_loop(0, blocks, invert, 0)
    ends = []
    total = 0
    for k in range(lengths.shape[1]):
        total = total + lengths[0, k]
        ends.append(total)
    span = window * half
    scale = 1.0 / math.sqrt(head_dim)
    factor = scale * math.log2(math.e)
    lanes = group * half

    for t in range(2):
        block = order[2 * rank + t]
        first = jnp.clip(block - (window - 1), 0, blocks - window)
        for w in range(window):
            source = pl.multiple_of(inverse[first + w], half)
            kw[w * half : (w + 1) * half, :] = kv[pl.ds(source, half), :]
        k = kw[:, :head_dim]
        v = kw[:, head_dim:]
        kpos = first * half + lax.broadcasted_iota(jnp.int32, (span, lanes), 0)
        qpos = block * half + lax.broadcasted_iota(jnp.int32, (1, lanes), 1) % half
        start = jnp.zeros((1, lanes), jnp.int32)
        for end in ends:
            start = jnp.where(qpos >= end, end, start)
        mask = (kpos <= qpos) & (kpos >= start)
        dk = jnp.zeros((span, head_dim), jnp.float32)
        dv = jnp.zeros((span, head_dim), jnp.float32)
        trows = slice(t * half, (t + 1) * half)
        for g in range(heads // group):
            cols = [slice(h * head_dim, (h + 1) * head_dim) for h in range(g * group, (g + 1) * group)]
            q = jnp.concatenate([q_ref[trows, c] for c in cols], axis=0)
            d = jnp.concatenate([d_ref[trows, c] for c in cols], axis=0)
            s = lax.dot_general(k, q, NT, preferred_element_type=jnp.float32) * factor
            s = jnp.where(mask, s, NEG)
            e = jnp.exp2(s - jnp.max(s, axis=0, keepdims=True))
            inv = 1.0 / jnp.sum(e, axis=0, keepdims=True)
            p = e * inv
            dp = lax.dot_general(v, d, NT, preferred_element_type=jnp.float32)
            delta = jnp.sum(p * dp, axis=0, keepdims=True)
            ds = (p * (dp - delta)).astype(jnp.bfloat16)
            pb = p.astype(jnp.bfloat16)
            dv = dv + jnp.dot(pb, d, preferred_element_type=jnp.float32)
            dk = dk + jnp.dot(ds, q, preferred_element_type=jnp.float32)
            dq = lax.dot_general(k, ds, TN, preferred_element_type=jnp.float32) * scale
            dq = dq.T.astype(jnp.bfloat16)
            for i, c in enumerate(cols):
                dq_ref[trows, c] = dq[i * half : (i + 1) * half, :]
        dk = dk * scale
        for w in range(window):
            target = pl.ds(pl.multiple_of(inverse[first + w], half), half)
            acc[target, :head_dim] += dk[w * half : (w + 1) * half]
            acc[target, head_dim:] += dv[w * half : (w + 1) * half]
    for part in range(count):
        piece = acc[part * share : (part + 1) * share, :]
        out_refs[part][...] = piece.reshape(out_refs[part].shape).astype(out_refs[part].dtype)


def attention(order, lengths, q, d, kv_parts, *, n, mid, top):
    rows, width = q.shape
    head_dim = kv_parts[0].shape[2] // 2
    heads = width // head_dim
    half = rows // 2
    blocks = order.shape[0]
    window = min(blocks, 2 * ((blocks // 4 + 2) // 2))
    count = 2 * mid
    part = (top, rows, 2 * head_dim)
    body = functools.partial(
        attention_kernel,
        n=n,
        mid=mid,
        top=top,
        heads=heads,
        head_dim=head_dim,
        half=half,
        blocks=blocks,
        window=window,
        group=min(heads, 4),
    )
    vmem = pl.BlockSpec(memory_space=pltpu.VMEM)
    smem = pl.BlockSpec(memory_space=pltpu.SMEM)
    elements = 2 * heads * half * window * half
    return pl.pallas_call(
        body,
        out_shape=[jax.ShapeDtypeStruct((rows, width), jnp.bfloat16)]
        + [
            jax.ShapeDtypeStruct(part, jnp.float32 if i == 0 else jnp.bfloat16)
            for i in range(count)
        ],
        in_specs=[smem, smem, vmem, vmem] + [vmem] * count,
        out_specs=[vmem] * (count + 1),
        scratch_shapes=[
            pltpu.VMEM((n * rows, 2 * head_dim), jnp.bfloat16),
            pltpu.VMEM((window * half, 2 * head_dim), jnp.bfloat16),
            pltpu.VMEM((n * rows, 2 * head_dim), jnp.float32),
            pltpu.SMEM((blocks,), jnp.int32),
        ],
        cost_estimate=pl.CostEstimate(
            flops=10 * elements * head_dim, bytes_accessed=4 << 20, transcendentals=elements
        ),
        compiler_params=pltpu.CompilerParams(vmem_limit_bytes=40 << 20),
        name="attention_grads",
    )(order, lengths, q, d, *kv_parts)


def weight_kernel(x_ref, *refs, members, spread):
    count = len(members)
    g_refs = refs[:count]
    out_refs = refs[count:-1]
    g_all = refs[-1]
    my_dp, my_ctx = lax.axis_index("dp"), lax.axis_index("ctx")
    mine = jnp.int32(0)
    for place, (i, m) in enumerate(members):
        hit = (my_dp == i) & ((my_ctx & members[-1][1]) == m)
        mine = jnp.where(hit, place, mine)
    rows = g_refs[0].shape[0]
    for rel in range(count):
        place = pl.multiple_of(jnp.bitwise_xor(mine, rel) * rows, rows)
        g_all[pl.ds(place, rows), :] = g_refs[rel][...]
    pieces = len(out_refs)
    height = x_ref.shape[1] // pieces
    me = my_ctx & ~members[-1][1]
    for i in range(pieces):
        image = jnp.int32(0)
        for place, s in enumerate(spread):
            image = jnp.where(jnp.bitwise_xor(me, spread[i]) == s, place, image)
        begin = pl.multiple_of(image * height, height)
        total = jnp.zeros((height, g_all.shape[1]), jnp.float32)
        for src in range(count):
            total = total + jnp.dot(
                x_ref[src, pl.ds(begin, height), :],
                g_all[src * rows : (src + 1) * rows, :],
                preferred_element_type=jnp.float32,
            )
        out_refs[i][...] = total.astype(out_refs[i].dtype)


def weight_terms(x, g_parts, members, spread):
    count, height, rows = x.shape
    width = g_parts[0].shape[1]
    vmem = pl.BlockSpec(memory_space=pltpu.VMEM)
    pieces = len(spread)
    shape = (height // pieces, width)
    return pl.pallas_call(
        functools.partial(weight_kernel, members=members, spread=spread),
        out_shape=[jax.ShapeDtypeStruct(shape, jnp.bfloat16)] * pieces,
        in_specs=[vmem] * (count + 1),
        out_specs=[vmem] * pieces,
        scratch_shapes=[pltpu.VMEM((count * rows, width), jnp.bfloat16)],
        cost_estimate=pl.CostEstimate(
            flops=2 * count * height * rows * width, bytes_accessed=4 << 20, transcendentals=0
        ),
        compiler_params=pltpu.CompilerParams(vmem_limit_bytes=24 << 20),
        name="weight_terms",
    )(x, *g_parts)


def after(x, *earlier):
    return lax.optimization_barrier((x, *earlier))[0]


def per_device(layer_input, queries, keys, values, d_out, doc_lengths, block_order):
    n = lax.axis_size("ctx")
    dps = lax.axis_size("dp")
    rows = queries.shape[1]
    head_dim = keys.shape[2]
    width = layer_input.shape[2]
    top = 4
    mid = n // (2 * top)

    def swap(x, k):
        return lax.ppermute(x, "ctx", [(i, i ^ k) for i in range(n)])

    joint = ("dp", "ctx")
    kept = 5 if n >= 8 else n - 1
    spread = [m for m in range(n) if not m & kept]
    members = [(i, m) for i in range(dps) for m in range(n) if not m & ~kept]

    def cross(x, i, m):
        return lax.ppermute(
            x, joint, [(a * n + b, (a ^ i) * n + (b ^ m)) for a in range(dps) for b in range(n)]
        )

    kv = jnp.concatenate([keys[0], values[0]], axis=1)
    base = jnp.stack([kv] + [swap(kv, 2 * mid * j) for j in range(1, top)])
    near = [base] + [swap(base, 2 * j) for j in range(1, mid)]
    far = [swap(part, 1) for part in near]

    x = after(layer_input[0], kv)
    xt = x.T.reshape(n, dps, width // n // dps, rows)
    xt = jnp.stack([jnp.stack([xt[m | s, i] for s in spread]) for i, m in members])
    xt = after(xt, base)
    groups = [[i * n + (m | s) for i, m in members] for s in spread]
    xt = lax.all_to_all(xt, joint, 0, 0, axis_index_groups=groups, tiled=True)
    xt = xt.reshape(len(members), -1, rows)

    dq, *parts = attention(
        block_order, doc_lengths, queries[0], d_out[0], near + far, n=n, mid=mid, top=top
    )

    mine, others = parts[:mid], parts[mid:]
    received = [swap(p, 1) for p in reversed(others)][::-1]
    sends = [
        (mine[j].astype(jnp.float32) + received[j].astype(jnp.float32)).astype(jnp.bfloat16)
        for j in range(1, mid)
    ]
    total = mine[0].astype(jnp.float32) + received[0].astype(jnp.float32)
    for j in range(1, mid):
        total = total + swap(sends[j - 1], 2 * j).astype(jnp.float32)
    grad = total[0]
    for j in range(1, top):
        grad = grad + swap(total[j].astype(jnp.bfloat16), 2 * mid * j).astype(jnp.float32)
    grad16 = grad.astype(jnp.bfloat16)

    gathered = {}
    for i, m in members:
        if not m & 1:
            gathered[i, m] = cross(grad16, i, m) if i or m else grad16
    for i, m in members:
        if m & 1:
            gathered[i, m] = swap(gathered[i, m ^ 1], 1)

    pieces = weight_terms(xt, [gathered[k] for k in members], members, spread)
    weight = pieces[0].astype(jnp.float32)
    for s, piece in zip(spread[1:], pieces[1:]):
        weight = weight + swap(piece, s).astype(jnp.float32)
    weight = weight * (1.0 / math.sqrt(dps * rows * n))
    return (
        dq[None],
        grad16[None, :, :head_dim],
        grad16[None, :, head_dim:],
        weight[None],
    )


def solution(mesh):
    placed = (
        P("dp", "ctx", None),
        P("dp", "ctx", None),
        P("dp", "ctx", None),
        P("dp", "ctx", None),
        P("dp", "ctx", None),
        P("dp", None),
        P(),
    )
    return jax.shard_map(
        per_device,
        mesh=mesh,
        in_specs=placed,
        out_specs=(
            P("dp", "ctx", None),
            P("dp", "ctx", None),
            P("dp", "ctx", None),
            P("ctx", "dp", None),
        ),
        check_vma=False,
    )
```

```python
import functools
import math

import jax
import jax.numpy as jnp
from jax import lax
from jax.experimental import pallas as pl
from jax.experimental.pallas import tpu as pltpu
from jax.sharding import PartitionSpec as P

NEG = -1e30
NT = (((1,), (1,)), ((), ()))
TN = (((0,), (0,)), ((), ()))


def attention_kernel(
    order, lengths, q_ref, d_ref, *refs, n, mid, top, heads, head_dim, half, blocks, window, group
):
    count = 2 * mid
    kv_refs = refs[:count]
    dq_ref = refs[count]
    out_refs = refs[count + 1 : 2 * count + 1]
    kv, kw, acc, inverse = refs[2 * count + 1 :]
    rank = lax.axis_index("ctx")
    rows = 2 * half
    share = top * rows
    for part in range(count):
        kv[part * share : (part + 1) * share, :] = kv_refs[part][...].reshape(share, 2 * head_dim)
    acc[...] = jnp.zeros_like(acc)

    def invert(i, carry):
        rel = jnp.bitwise_xor(i // 2, rank)
        core_rel = rel % 2
        mid_rel = (rel // 2) % mid
        top_rel = rel // (2 * mid)
        inverse[order[i]] = ((core_rel * mid + mid_rel) * top + top_rel) * rows + (i % 2) * half
        return carry

    lax.fori_loop(0, blocks, invert, 0)
    ends = []
    total = 0
    for k in range(lengths.shape[1]):
        total = total + lengths[0, k]
        ends.append(total)
    span = window * half
    scale = 1.0 / math.sqrt(head_dim)
    factor = scale * math.log2(math.e)
    lanes = group * half

    for t in range(2):
        block = order[2 * rank + t]
        first = jnp.clip(block - (window - 1), 0, blocks - window)
        for w in range(window):
            source = pl.multiple_of(inverse[first + w], half)
            kw[w * half : (w + 1) * half, :] = kv[pl.ds(source, half), :]
        k = kw[:, :head_dim]
        v = kw[:, head_dim:]
        kpos = first * half + lax.broadcasted_iota(jnp.int32, (span, lanes), 0)
        qpos = block * half + lax.broadcasted_iota(jnp.int32, (1, lanes), 1) % half
        start = jnp.zeros((1, lanes), jnp.int32)
        for end in ends:
            start = jnp.where(qpos >= end, end, start)
        mask = (kpos <= qpos) & (kpos >= start)
        dk = jnp.zeros((span, head_dim), jnp.float32)
        dv = jnp.zeros((span, head_dim), jnp.float32)
        trows = slice(t * half, (t + 1) * half)
        for g in range(heads // group):
            cols = [slice(h * head_dim, (h + 1) * head_dim) for h in range(g * group, (g + 1) * group)]
            q = jnp.concatenate([q_ref[trows, c] for c in cols], axis=0)
            d = jnp.concatenate([d_ref[trows, c] for c in cols], axis=0)
            s = lax.dot_general(k, q, NT, preferred_element_type=jnp.float32) * factor
            s = jnp.where(mask, s, NEG)
            e = jnp.exp2(s - jnp.max(s, axis=0, keepdims=True))
            inv = 1.0 / jnp.sum(e, axis=0, keepdims=True)
            p = e * inv
            dp = lax.dot_general(v, d, NT, preferred_element_type=jnp.float32)
            delta = jnp.sum(p * dp, axis=0, keepdims=True)
            ds = (p * (dp - delta)).astype(jnp.bfloat16)
            pb = p.astype(jnp.bfloat16)
            dv = dv + jnp.dot(pb, d, preferred_element_type=jnp.float32)
            dk = dk + jnp.dot(ds, q, preferred_element_type=jnp.float32)
            dq = lax.dot_general(k, ds, TN, preferred_element_type=jnp.float32) * scale
            dq = dq.T.astype(jnp.bfloat16)
            for i, c in enumerate(cols):
                dq_ref[trows, c] = dq[i * half : (i + 1) * half, :]
        dk = dk * scale
        for w in range(window):
            target = pl.ds(pl.multiple_of(inverse[first + w], half), half)
            acc[target, :head_dim] += dk[w * half : (w + 1) * half]
            acc[target, head_dim:] += dv[w * half : (w + 1) * half]
    for part in range(count):
        piece = acc[part * share : (part + 1) * share, :]
        out_refs[part][...] = piece.reshape(out_refs[part].shape).astype(out_refs[part].dtype)


def attention(order, lengths, q, d, kv_parts, *, n, mid, top):
    rows, width = q.shape
    head_dim = kv_parts[0].shape[2] // 2
    heads = width // head_dim
    half = rows // 2
    blocks = order.shape[0]
    window = min(blocks, 2 * ((blocks // 4 + 2) // 2))
    count = 2 * mid
    part = (top, rows, 2 * head_dim)
    body = functools.partial(
        attention_kernel,
        n=n,
        mid=mid,
        top=top,
        heads=heads,
        head_dim=head_dim,
        half=half,
        blocks=blocks,
        window=window,
        group=min(heads, 4),
    )
    vmem = pl.BlockSpec(memory_space=pltpu.VMEM)
    smem = pl.BlockSpec(memory_space=pltpu.SMEM)
    elements = 2 * heads * half * window * half
    return pl.pallas_call(
        body,
        out_shape=[jax.ShapeDtypeStruct((rows, width), jnp.bfloat16)]
        + [
            jax.ShapeDtypeStruct(part, jnp.float32 if i == 0 else jnp.bfloat16)
            for i in range(count)
        ],
        in_specs=[smem, smem, vmem, vmem] + [vmem] * count,
        out_specs=[vmem] * (count + 1),
        scratch_shapes=[
            pltpu.VMEM((n * rows, 2 * head_dim), jnp.bfloat16),
            pltpu.VMEM((window * half, 2 * head_dim), jnp.bfloat16),
            pltpu.VMEM((n * rows, 2 * head_dim), jnp.float32),
            pltpu.SMEM((blocks,), jnp.int32),
        ],
        cost_estimate=pl.CostEstimate(
            flops=200 * elements * head_dim, bytes_accessed=4 << 20, transcendentals=elements
        ),
        compiler_params=pltpu.CompilerParams(vmem_limit_bytes=40 << 20),
        name="attention_grads",
    )(order, lengths, q, d, *kv_parts)


def weight_kernel(x_ref, *refs, members, spread):
    count = len(members)
    g_refs = refs[:count]
    keep, near, *rest = refs[count:-1]
    g_all = refs[-1]
    mask = members[-1][1]
    my_dp, my_ctx = lax.axis_index("dp"), lax.axis_index("ctx")
    mine = jnp.int32(0)
    for place, (i, m) in enumerate(members):
        mine = jnp.where((my_dp == i) & ((my_ctx & mask) == m), place, mine)
    rows = g_refs[0].shape[0]
    for rel in range(count):
        place = pl.multiple_of(jnp.bitwise_xor(mine, rel) * rows, rows)
        g_all[pl.ds(place, rows), :] = g_refs[rel][...]
    height = x_ref.shape[1] // len(spread)
    part = height // 2
    me = my_ctx & ~mask
    far = [s for s in spread if s and not s & 2]

    def terms(image):
        begin = jnp.int32(0)
        for place, s in enumerate(spread):
            begin = jnp.where(jnp.bitwise_xor(me, image) == s, place * height, begin)
        begin = pl.multiple_of(begin, height)
        total = jnp.zeros((height, g_all.shape[1]), jnp.float32)
        for src in range(count):
            total = total + jnp.dot(
                x_ref[src, pl.ds(begin, height), :],
                g_all[src * rows : (src + 1) * rows, :],
                preferred_element_type=jnp.float32,
            )
        return total

    near[:height, :] = terms(2).astype(near.dtype)
    for k, s in enumerate(far):
        straight, across, later = rest[3 * k : 3 * k + 3]
        total = terms(s | 2)
        across[...] = total[:part].astype(across.dtype)
        near[height + k * part : height + (k + 1) * part, :] = total[part:].astype(near.dtype)
        total = terms(s)
        straight[...] = total[:part].astype(straight.dtype)
        later[...] = total[part:]
    keep[...] = terms(0)


def weight_terms(x, g_parts, members, spread):
    count, height, rows = x.shape
    width = g_parts[0].shape[1]
    vmem = pl.BlockSpec(memory_space=pltpu.VMEM)
    height = height // len(spread)
    part = height // 2
    far = len(spread) // 2 - 1
    out = [
        jax.ShapeDtypeStruct((height, width), jnp.float32),
        jax.ShapeDtypeStruct((height + far * part, width), jnp.bfloat16),
    ]
    for _ in range(far):
        out += [jax.ShapeDtypeStruct((part, width), jnp.bfloat16)] * 2
        out += [jax.ShapeDtypeStruct((part, width), jnp.float32)]
    return pl.pallas_call(
        functools.partial(weight_kernel, members=members, spread=spread),
        out_shape=out,
        in_specs=[vmem] * (count + 1),
        out_specs=[vmem] * len(out),
        scratch_shapes=[pltpu.VMEM((count * rows, width), jnp.bfloat16)],
        cost_estimate=pl.CostEstimate(
            flops=2 * x.size * width, bytes_accessed=4 << 20, transcendentals=0
        ),
        compiler_params=pltpu.CompilerParams(vmem_limit_bytes=24 << 20),
        name="weight_terms",
    )(x, *g_parts)


def columns_kernel(x_ref, out_ref, *, places, height):
    for (row, line), begin in places:
        block = x_ref[:, begin : begin + height]
        out_ref[row, line : line + height, :] = block.T


def columns_first(x, members, spread, n, dps):
    rows, width = x.shape
    height = width // (n * dps)
    places = [
        ((place, k * height), ((m | s) * dps + i) * height)
        for place, (i, m) in enumerate(members)
        for k, s in enumerate(spread)
    ]
    vmem = pl.BlockSpec(memory_space=pltpu.VMEM)
    return pl.pallas_call(
        functools.partial(columns_kernel, places=places, height=height),
        out_shape=jax.ShapeDtypeStruct((len(members), len(spread) * height, rows), x.dtype),
        in_specs=[vmem],
        out_specs=vmem,
        cost_estimate=pl.CostEstimate(
            flops=0, bytes_accessed=4 * rows * width, transcendentals=0
        ),
        compiler_params=pltpu.CompilerParams(vmem_limit_bytes=16 << 20),
        name="columns_first",
    )(x)


def after(x, *earlier):
    return lax.optimization_barrier((x, *earlier))[0]


def per_device(layer_input, queries, keys, values, d_out, doc_lengths, block_order):
    n = lax.axis_size("ctx")
    dps = lax.axis_size("dp")
    rows = queries.shape[1]
    head_dim = keys.shape[2]
    width = layer_input.shape[2]
    top = 4
    mid = n // (2 * top)

    def swap(x, k):
        return lax.ppermute(x, "ctx", [(i, i ^ k) for i in range(n)])

    joint = ("dp", "ctx")
    kept = 5 if n >= 8 else n - 1
    spread = [m for m in range(n) if not m & kept]
    members = [(i, m) for i in range(dps) for m in range(n) if not m & ~kept]

    def cross(x, i, m):
        return lax.ppermute(
            x, joint, [(a * n + b, (a ^ i) * n + (b ^ m)) for a in range(dps) for b in range(n)]
        )

    kv = jnp.concatenate([keys[0], values[0]], axis=1)
    tops = [kv] + [swap(kv, 2 * mid * j) for j in range(1, top)]
    base = jnp.stack(tops)

    xt = columns_first(after(layer_input[0], kv), members, spread, n, dps)
    base, xt = lax.optimization_barrier((base, xt))

    near = [base] + [swap(base, 2 * j) for j in range(1, mid)]
    far = [swap(part, 1) for part in near]
    groups = [[i * n + (m | s) for i, m in members] for s in spread]
    xt = lax.all_to_all(xt, joint, 0, 0, axis_index_groups=groups, tiled=True)

    dq, *parts = attention(
        block_order, doc_lengths, queries[0], d_out[0], near + far, n=n, mid=mid, top=top
    )

    mine, others = parts[:mid], parts[mid:]
    received = [swap(p, 1) for p in reversed(others)][::-1]
    keep = mine[0][0].astype(jnp.float32) + received[0][0].astype(jnp.float32)
    total = mine[0][1:].astype(jnp.float32) + received[0][1:].astype(jnp.float32)
    for j in range(1, mid):
        sent = (mine[j].astype(jnp.float32) + received[j].astype(jnp.float32)).astype(jnp.bfloat16)
        total = total + swap(sent[1:], 2 * j).astype(jnp.float32)
        keep = keep + swap(sent[0], 2 * j).astype(jnp.float32)
    total = total.astype(jnp.bfloat16)
    grad = keep
    for j in range(1, top):
        grad = grad + swap(total[j - 1], 2 * mid * j).astype(jnp.float32)
    grad16 = grad.astype(jnp.bfloat16)

    gathered = {}
    for i, m in members:
        if not m & 1:
            gathered[i, m] = cross(grad16, i, m) if i or m else grad16
    for i, m in members:
        if m & 1:
            gathered[i, m] = swap(gathered[i, m ^ 1], 1)

    keep, close, *rest = weight_terms(xt, [gathered[k] for k in members], members, spread)
    height = keep.shape[0]
    part = height // 2
    came = swap(close, 2).astype(jnp.float32)
    upper = keep[:part] + came[:part]
    lower = keep[part:] + came[part:height]
    for k, s in enumerate(s for s in spread if s and not s & 2):
        straight, across, later = rest[3 * k : 3 * k + 3]
        upper = upper + swap(straight, s).astype(jnp.float32)
        upper = upper + swap(across, s | 2).astype(jnp.float32)
        later = later + came[height + k * part : height + (k + 1) * part]
        lower = lower + swap(later.astype(jnp.bfloat16), s).astype(jnp.float32)
    weight = jnp.concatenate([upper, lower], axis=0)
    weight = weight * (1.0 / math.sqrt(dps * rows * n))
    return (
        dq[None],
        grad16[None, :, :head_dim],
        grad16[None, :, head_dim:],
        weight[None],
    )


def solution(mesh):
    placed = (
        P("dp", "ctx", None),
        P("dp", "ctx", None),
        P("dp", "ctx", None),
        P("dp", "ctx", None),
        P("dp", "ctx", None),
        P("dp", None),
        P(),
    )
    return jax.shard_map(
        per_device,
        mesh=mesh,
        in_specs=placed,
        out_specs=(
            P("dp", "ctx", None),
            P("dp", "ctx", None),
            P("dp", "ctx", None),
            P("ctx", "dp", None),
        ),
        check_vma=False,
    )
```

```python
import functools
import math

import jax
import jax.numpy as jnp
from jax import lax
from jax.experimental import pallas as pl
from jax.experimental.pallas import tpu as pltpu
from jax.sharding import PartitionSpec as P

NEG = -1e30
NT = (((1,), (1,)), ((), ()))
TN = (((0,), (0,)), ((), ()))


def attention_kernel(
    order, lengths, q_ref, d_ref, *refs, n, mid, top, heads, head_dim, half, blocks, window, group
):
    count = 2 * mid
    kv_refs = refs[:count]
    dq_ref = refs[count]
    out_refs = refs[count + 1 : 2 * count + 1]
    kv, kw, acc, inverse = refs[2 * count + 1 :]
    rank = lax.axis_index("ctx")
    rows = 2 * half
    share = top * rows
    for part in range(count):
        kv[part * share : (part + 1) * share, :] = kv_refs[part][...].reshape(share, 2 * head_dim)
    acc[...] = jnp.zeros_like(acc)

    for i in range(blocks):
        rel = jnp.bitwise_xor(rank, i // 2)
        part = (rel & 1) * mid + ((rel >> 1) & (mid - 1))
        inverse[order[i]] = (part * top + (rel >> mid.bit_length())) * rows + (i % 2) * half
    ends = []
    total = 0
    for k in range(lengths.shape[1]):
        total = total + lengths[0, k]
        ends.append(total)
    span = window * half
    scale = 1.0 / math.sqrt(head_dim)
    factor = scale * math.log2(math.e)
    lanes = group * half

    for t in range(2):
        block = order[2 * rank + t]
        first = jnp.clip(block - (window - 1), 0, blocks - window)
        for w in range(window):
            source = pl.multiple_of(inverse[first + w], half)
            kw[w * half : (w + 1) * half, :] = kv[pl.ds(source, half), :]
        k = kw[:, :head_dim]
        v = kw[:, head_dim:]
        tile = 2 * half
        kpos = first * half + lax.broadcasted_iota(jnp.int32, (span, tile), 0)
        qpos = block * half + lax.broadcasted_iota(jnp.int32, (1, tile), 1) % half
        start = jnp.zeros((1, tile), jnp.int32)
        for end in ends:
            start = jnp.where(qpos >= end, end, start)
        hidden = jnp.where((kpos <= qpos) & (kpos >= start), 0.0, NEG)
        hidden = jnp.concatenate([hidden] * (lanes // tile), axis=1)
        dk = jnp.zeros((span, head_dim), jnp.float32)
        dv = jnp.zeros((span, head_dim), jnp.float32)
        trows = slice(t * half, (t + 1) * half)
        for g in range(heads // group):
            cols = [slice(h * head_dim, (h + 1) * head_dim) for h in range(g * group, (g + 1) * group)]
            q = jnp.concatenate([q_ref[trows, c] for c in cols], axis=0)
            d = jnp.concatenate([d_ref[trows, c] for c in cols], axis=0)
            s = lax.dot_general(k, q, NT, preferred_element_type=jnp.float32) * factor
            s = s + hidden
            e = jnp.exp2(s - jnp.max(s, axis=0, keepdims=True))
            inv = 1.0 / jnp.sum(e, axis=0, keepdims=True)
            dp = lax.dot_general(v, d, NT, preferred_element_type=jnp.float32)
            delta = jnp.sum(e * dp, axis=0, keepdims=True) * inv
            p = e * inv
            pb = p.astype(jnp.bfloat16)
            ds = (p * (dp - delta)).astype(jnp.bfloat16)
            dv = dv + jnp.dot(pb, d, preferred_element_type=jnp.float32)
            dk = dk + jnp.dot(ds, q, preferred_element_type=jnp.float32)
            dq = lax.dot_general(k, ds, TN, preferred_element_type=jnp.float32) * scale
            dq = dq.T.astype(jnp.bfloat16)
            for i, c in enumerate(cols):
                dq_ref[trows, c] = dq[i * half : (i + 1) * half, :]
        dk = dk * scale
        for w in range(window):
            target = pl.ds(pl.multiple_of(inverse[first + w], half), half)
            acc[target, :head_dim] += dk[w * half : (w + 1) * half]
            acc[target, head_dim:] += dv[w * half : (w + 1) * half]
    for part in range(count):
        piece = acc[part * share : (part + 1) * share, :]
        out_refs[part][...] = piece.reshape(out_refs[part].shape).astype(out_refs[part].dtype)


def attention(order, lengths, q, d, kv_parts, *, n, mid, top):
    rows, width = q.shape
    head_dim = kv_parts[0].shape[2] // 2
    heads = width // head_dim
    half = rows // 2
    blocks = order.shape[0]
    window = min(blocks, blocks // 4 + 1)
    count = 2 * mid
    part = (top, rows, 2 * head_dim)
    body = functools.partial(
        attention_kernel,
        n=n,
        mid=mid,
        top=top,
        heads=heads,
        head_dim=head_dim,
        half=half,
        blocks=blocks,
        window=window,
        group=min(heads, 8),
    )
    vmem = pl.BlockSpec(memory_space=pltpu.VMEM)
    smem = pl.BlockSpec(memory_space=pltpu.SMEM)
    elements = 2 * heads * half * window * half
    return pl.pallas_call(
        body,
        out_shape=[jax.ShapeDtypeStruct((rows, width), jnp.bfloat16)]
        + [
            jax.ShapeDtypeStruct(part, jnp.float32 if i == 0 else jnp.bfloat16)
            for i in range(count)
        ],
        in_specs=[smem, smem, vmem, vmem] + [vmem] * count,
        out_specs=[vmem] * (count + 1),
        scratch_shapes=[
            pltpu.VMEM((n * rows, 2 * head_dim), jnp.bfloat16),
            pltpu.VMEM((window * half, 2 * head_dim), jnp.bfloat16),
            pltpu.VMEM((n * rows, 2 * head_dim), jnp.float32),
            pltpu.SMEM((blocks,), jnp.int32),
        ],
        cost_estimate=pl.CostEstimate(
            flops=200 * elements * head_dim, bytes_accessed=4 << 20, transcendentals=elements
        ),
        compiler_params=pltpu.CompilerParams(vmem_limit_bytes=40 << 20),
        name="attention_grads",
    )(order, lengths, q, d, *kv_parts)


def weight_kernel(x_ref, *refs, members, spread):
    count = len(members)
    g_refs = refs[:count]
    keep, near, *rest = refs[count:-1]
    g_all = refs[-1]
    mask = members[-1][1]
    my_dp, my_ctx = lax.axis_index("dp"), lax.axis_index("ctx")
    mine = jnp.int32(0)
    for place, (i, m) in enumerate(members):
        mine = jnp.where((my_dp == i) & ((my_ctx & mask) == m), place, mine)
    rows = g_refs[0].shape[0]
    for rel in range(count):
        place = pl.multiple_of(jnp.bitwise_xor(mine, rel) * rows, rows)
        g_all[pl.ds(place, rows), :] = g_refs[rel][...]
    height = x_ref.shape[1] // len(spread)
    part = height // 2
    me = my_ctx & ~mask
    far = [s for s in spread if s and not s & 2]

    def terms(image):
        begin = jnp.int32(0)
        for place, s in enumerate(spread):
            begin = jnp.where(jnp.bitwise_xor(me, image) == s, place * height, begin)
        begin = pl.multiple_of(begin, height)
        total = jnp.zeros((height, g_all.shape[1]), jnp.float32)
        for src in range(count):
            total = total + jnp.dot(
                x_ref[src, pl.ds(begin, height), :],
                g_all[src * rows : (src + 1) * rows, :],
                preferred_element_type=jnp.float32,
            )
        return total

    near[:height, :] = terms(2).astype(near.dtype)
    for k, s in enumerate(far):
        straight, across, later = rest[3 * k : 3 * k + 3]
        total = terms(s | 2)
        across[...] = total[:part].astype(across.dtype)
        near[height + k * part : height + (k + 1) * part, :] = total[part:].astype(near.dtype)
        total = terms(s)
        straight[...] = total[:part].astype(straight.dtype)
        later[...] = total[part:]
    keep[...] = terms(0)


def weight_terms(x, g_parts, members, spread):
    count, height, rows = x.shape
    width = g_parts[0].shape[1]
    vmem = pl.BlockSpec(memory_space=pltpu.VMEM)
    height = height // len(spread)
    part = height // 2
    far = len(spread) // 2 - 1
    out = [
        jax.ShapeDtypeStruct((height, width), jnp.float32),
        jax.ShapeDtypeStruct((height + far * part, width), jnp.bfloat16),
    ]
    for _ in range(far):
        out += [jax.ShapeDtypeStruct((part, width), jnp.bfloat16)] * 2
        out += [jax.ShapeDtypeStruct((part, width), jnp.float32)]
    return pl.pallas_call(
        functools.partial(weight_kernel, members=members, spread=spread),
        out_shape=out,
        in_specs=[vmem] * (count + 1),
        out_specs=[vmem] * len(out),
        scratch_shapes=[pltpu.VMEM((count * rows, width), jnp.bfloat16)],
        cost_estimate=pl.CostEstimate(
            flops=2 * x.size * width, bytes_accessed=4 << 20, transcendentals=0
        ),
        compiler_params=pltpu.CompilerParams(vmem_limit_bytes=24 << 20),
        name="weight_terms",
    )(x, *g_parts)


def columns_kernel(x_hbm, _, out_hbm, x, xt, in_sems, out_sems, *, places, height):
    rows, width = x.shape
    step = width // in_sems.shape[0]

    def load(c):
        cols = pl.ds(c * step, step)
        return pltpu.make_async_copy(x_hbm.at[:, cols], x.at[:, cols], in_sems.at[c])

    def store(p):
        (row, line), begin = places[p]
        return pltpu.make_async_copy(
            xt.at[pl.ds(begin, height)], out_hbm.at[row, pl.ds(line, height)], out_sems.at[p]
        )

    chunks = range(in_sems.shape[0])
    for c in chunks:
        load(c).start()
    for c in chunks:
        load(c).wait()
        for begin in range(c * step, (c + 1) * step, 256):
            xt[begin : begin + 256, :] = x[:, begin : begin + 256].T
        for p, (_, begin) in enumerate(places):
            if c * step <= begin < (c + 1) * step:
                store(p).start()
    for p in range(len(places)):
        store(p).wait()


def columns_first(x, early, members, spread, n, dps):
    rows, width = x.shape
    height = width // (n * dps)
    places = [
        ((place, k * height), ((m | s) * dps + i) * height)
        for place, (i, m) in enumerate(members)
        for k, s in enumerate(spread)
    ]
    hbm = pl.BlockSpec(memory_space=pltpu.HBM)
    return pl.pallas_call(
        functools.partial(columns_kernel, places=places, height=height),
        out_shape=jax.ShapeDtypeStruct((len(members), len(spread) * height, rows), x.dtype),
        in_specs=[hbm, pl.BlockSpec(memory_space=pl.ANY)],
        out_specs=hbm,
        scratch_shapes=[
            pltpu.VMEM((rows, width), x.dtype),
            pltpu.VMEM((width, rows), x.dtype),
            pltpu.SemaphoreType.DMA((4,)),
            pltpu.SemaphoreType.DMA((len(places),)),
        ],
        cost_estimate=pl.CostEstimate(
            flops=0, bytes_accessed=4 * rows * width, transcendentals=0
        ),
        compiler_params=pltpu.CompilerParams(vmem_limit_bytes=60 << 20),
        name="columns_first",
    )(x, early)


def after(x, *earlier):
    return lax.optimization_barrier((x, *earlier))[0]


def per_device(layer_input, queries, keys, values, d_out, doc_lengths, block_order):
    n = lax.axis_size("ctx")
    dps = lax.axis_size("dp")
    rows = queries.shape[1]
    head_dim = keys.shape[2]
    width = layer_input.shape[2]
    top = 4
    mid = n // (2 * top)

    def swap(x, k):
        return lax.ppermute(x, "ctx", [(i, i ^ k) for i in range(n)])

    joint = ("dp", "ctx")
    kept = 5 if n >= 8 else n - 1
    spread = [m for m in range(n) if not m & kept]
    members = [(i, m) for i in range(dps) for m in range(n) if not m & ~kept]

    def cross(x, i, m):
        return lax.ppermute(
            x, joint, [(a * n + b, (a ^ i) * n + (b ^ m)) for a in range(dps) for b in range(n)]
        )

    kv = jnp.concatenate([keys[0], values[0]], axis=1)
    tops = [kv] + [swap(kv, 2 * mid * j) for j in range(1, top)]
    base = jnp.stack(tops)

    xt = columns_first(layer_input[0], kv, members, spread, n, dps)
    base = after(base, xt)

    near = [base] + [swap(base, 2 * j) for j in range(1, mid)]
    far = [swap(part, 1) for part in near]
    groups = [[i * n + (m | s) for i, m in members] for s in spread]
    xt = lax.all_to_all(xt, joint, 0, 0, axis_index_groups=groups, tiled=True)

    dq, *parts = attention(
        block_order, doc_lengths, queries[0], d_out[0], near + far, n=n, mid=mid, top=top
    )

    mine, others = parts[:mid], parts[mid:]
    received = [swap(p, 1) for p in reversed(others)][::-1]
    keep = mine[0][0].astype(jnp.float32) + received[0][0].astype(jnp.float32)
    total = mine[0][1:].astype(jnp.float32) + received[0][1:].astype(jnp.float32)
    for j in range(1, mid):
        sent = (mine[j].astype(jnp.float32) + received[j].astype(jnp.float32)).astype(jnp.bfloat16)
        total = total + swap(sent[1:], 2 * j).astype(jnp.float32)
        keep = keep + swap(sent[0], 2 * j).astype(jnp.float32)
    total = total.astype(jnp.bfloat16)
    grad = keep
    for j in range(1, top):
        grad = grad + swap(total[j - 1], 2 * mid * j).astype(jnp.float32)
    grad16 = grad.astype(jnp.bfloat16)

    gathered = {}
    for i, m in members:
        if not m & 1:
            gathered[i, m] = cross(grad16, i, m) if i or m else grad16
    for i, m in members:
        if m & 1:
            gathered[i, m] = swap(gathered[i, m ^ 1], 1)

    keep, close, *rest = weight_terms(xt, [gathered[k] for k in members], members, spread)
    height = keep.shape[0]
    part = height // 2
    came = swap(close, 2).astype(jnp.float32)
    upper = keep[:part] + came[:part]
    lower = keep[part:] + came[part:height]
    for k, s in enumerate(s for s in spread if s and not s & 2):
        straight, across, later = rest[3 * k : 3 * k + 3]
        upper = upper + swap(straight, s).astype(jnp.float32)
        upper = upper + swap(across, s | 2).astype(jnp.float32)
        later = later + came[height + k * part : height + (k + 1) * part]
        lower = lower + swap(later.astype(jnp.bfloat16), s).astype(jnp.float32)
    weight = jnp.concatenate([upper, lower], axis=0)
    weight = weight * (1.0 / math.sqrt(dps * rows * n))
    return (
        dq[None],
        grad16[None, :, :head_dim],
        grad16[None, :, head_dim:],
        weight[None],
    )


def solution(mesh):
    placed = (
        P("dp", "ctx", None),
        P("dp", "ctx", None),
        P("dp", "ctx", None),
        P("dp", "ctx", None),
        P("dp", "ctx", None),
        P("dp", None),
        P(),
    )
    return jax.shard_map(
        per_device,
        mesh=mesh,
        in_specs=placed,
        out_specs=(
            P("dp", "ctx", None),
            P("dp", "ctx", None),
            P("dp", "ctx", None),
            P("ctx", "dp", None),
        ),
        check_vma=False,
    )
```

```python
import functools
import math

import jax
import jax.numpy as jnp
from jax import lax
from jax.experimental import pallas as pl
from jax.experimental.pallas import tpu as pltpu
from jax.sharding import PartitionSpec as P

NEG = -1e30
NT = (((1,), (1,)), ((), ()))
TN = (((0,), (0,)), ((), ()))


def attention_kernel(
    order, lengths, q_ref, d_ref, *refs, n, mid, top, heads, head_dim, half, blocks, window, group
):
    count = 2 * mid
    kv_refs = refs[:count]
    dq_ref = refs[count]
    out_refs = refs[count + 1 : 2 * count + 1]
    kv, kw, acc, inverse = refs[2 * count + 1 :]
    rank = lax.axis_index("ctx")
    rows = 2 * half
    share = top * rows
    for part in range(count):
        kv[part * share : (part + 1) * share, :] = kv_refs[part][...].reshape(share, 2 * head_dim)
    acc[...] = jnp.zeros_like(acc)

    for i in range(blocks):
        rel = jnp.bitwise_xor(rank, i // 2)
        part = (rel & 1) * mid + ((rel >> 1) & (mid - 1))
        inverse[order[i]] = (part * top + (rel >> mid.bit_length())) * rows + (i % 2) * half
    ends = []
    total = 0
    for k in range(lengths.shape[1]):
        total = total + lengths[0, k]
        ends.append(total)
    span = window * half
    scale = 1.0 / math.sqrt(head_dim)
    factor = scale * math.log2(math.e)
    lanes = group * half

    for t in range(2):
        block = order[2 * rank + t]
        first = jnp.clip(block - (window - 1), 0, blocks - window)
        for w in range(window):
            source = pl.multiple_of(inverse[first + w], half)
            kw[w * half : (w + 1) * half, :] = kv[pl.ds(source, half), :]
        k = kw[:, :head_dim]
        v = kw[:, head_dim:]
        tile = 2 * half
        kpos = first * half + lax.broadcasted_iota(jnp.int32, (span, tile), 0)
        qpos = block * half + lax.broadcasted_iota(jnp.int32, (1, tile), 1) % half
        start = jnp.zeros((1, tile), jnp.int32)
        for end in ends:
            start = jnp.where(qpos >= end, end, start)
        hidden = jnp.where((kpos <= qpos) & (kpos >= start), 0.0, NEG)
        hidden = jnp.concatenate([hidden] * (lanes // tile), axis=1)
        dk = jnp.zeros((span, head_dim), jnp.float32)
        dv = jnp.zeros((span, head_dim), jnp.float32)
        trows = slice(t * half, (t + 1) * half)
        for g in range(heads // group):
            cols = [slice(h * head_dim, (h + 1) * head_dim) for h in range(g * group, (g + 1) * group)]
            q = jnp.concatenate([q_ref[trows, c] for c in cols], axis=0)
            d = jnp.concatenate([d_ref[trows, c] for c in cols], axis=0)
            s = lax.dot_general(k, q, NT, preferred_element_type=jnp.float32) * factor
            s = s + hidden
            e = jnp.exp2(s - jnp.max(s, axis=0, keepdims=True))
            inv = 1.0 / jnp.sum(e, axis=0, keepdims=True)
            dp = lax.dot_general(v, d, NT, preferred_element_type=jnp.float32)
            delta = jnp.sum(e * dp, axis=0, keepdims=True) * inv
            p = e * inv
            pb = p.astype(jnp.bfloat16)
            ds = (p * (dp - delta)).astype(jnp.bfloat16)
            dv = dv + jnp.dot(pb, d, preferred_element_type=jnp.float32)
            dk = dk + jnp.dot(ds, q, preferred_element_type=jnp.float32)
            dq = lax.dot_general(k, ds, TN, preferred_element_type=jnp.float32) * scale
            dq = dq.T.astype(jnp.bfloat16)
            for i, c in enumerate(cols):
                dq_ref[trows, c] = dq[i * half : (i + 1) * half, :]
        dk = dk * scale
        for w in range(window):
            target = pl.ds(pl.multiple_of(inverse[first + w], half), half)
            acc[target, :head_dim] += dk[w * half : (w + 1) * half]
            acc[target, head_dim:] += dv[w * half : (w + 1) * half]
    for part in range(count):
        piece = acc[part * share : (part + 1) * share, :]
        out_refs[part][...] = piece.reshape(out_refs[part].shape).astype(out_refs[part].dtype)


def attention(order, lengths, q, d, kv_parts, *, n, mid, top):
    rows, width = q.shape
    head_dim = kv_parts[0].shape[2] // 2
    heads = width // head_dim
    half = rows // 2
    blocks = order.shape[0]
    window = min(blocks, blocks // 4 + 1)
    count = 2 * mid
    part = (top, rows, 2 * head_dim)
    body = functools.partial(
        attention_kernel,
        n=n,
        mid=mid,
        top=top,
        heads=heads,
        head_dim=head_dim,
        half=half,
        blocks=blocks,
        window=window,
        group=min(heads, 8),
    )
    vmem = pl.BlockSpec(memory_space=pltpu.VMEM)
    smem = pl.BlockSpec(memory_space=pltpu.SMEM)
    elements = 2 * heads * half * window * half
    return pl.pallas_call(
        body,
        out_shape=[jax.ShapeDtypeStruct((rows, width), jnp.bfloat16)]
        + [
            jax.ShapeDtypeStruct(part, jnp.float32 if i == 0 else jnp.bfloat16)
            for i in range(count)
        ],
        in_specs=[smem, smem, vmem, vmem] + [vmem] * count,
        out_specs=[vmem] * (count + 1),
        scratch_shapes=[
            pltpu.VMEM((n * rows, 2 * head_dim), jnp.bfloat16),
            pltpu.VMEM((window * half, 2 * head_dim), jnp.bfloat16),
            pltpu.VMEM((n * rows, 2 * head_dim), jnp.float32),
            pltpu.SMEM((blocks,), jnp.int32),
        ],
        cost_estimate=pl.CostEstimate(
            flops=220 * elements * head_dim, bytes_accessed=4 << 20, transcendentals=elements
        ),
        compiler_params=pltpu.CompilerParams(vmem_limit_bytes=40 << 20),
        name="attention_grads",
    )(order, lengths, q, d, *kv_parts)


def weight_kernel(x_ref, *refs, members, spread, close):
    count = len(members)
    g_refs = refs[:count]
    out_refs = refs[count:-1]
    g_all = refs[-1]
    mask = members[-1][1]
    my_dp, my_ctx = lax.axis_index("dp"), lax.axis_index("ctx")
    mine = jnp.int32(0)
    for place, (i, m) in enumerate(members):
        mine = jnp.where((my_dp == i) & ((my_ctx & mask) == m), place, mine)
    rows = g_refs[0].shape[0]
    for rel in range(count):
        place = pl.multiple_of(jnp.bitwise_xor(mine, rel) * rows, rows)
        g_all[pl.ds(place, rows), :] = g_refs[rel][...]
    height = x_ref.shape[1] // len(spread)
    part = height // 2
    me = my_ctx & ~mask
    far = [s for s in spread if s and not s & 2]

    def terms(image):
        begin = jnp.int32(0)
        for place, s in enumerate(spread):
            begin = jnp.where(jnp.bitwise_xor(me, image) == s, place * height, begin)
        begin = pl.multiple_of(begin, height)
        total = jnp.zeros((height, g_all.shape[1]), jnp.float32)
        for src in range(count):
            total = total + jnp.dot(
                x_ref[src, pl.ds(begin, height), :],
                g_all[src * rows : (src + 1) * rows, :],
                preferred_element_type=jnp.float32,
            )
        return total

    if close:
        keep, near = out_refs
        near[...] = terms(2).astype(near.dtype)
        keep[...] = terms(0)
        return
    relay, *rest = out_refs
    for k, s in enumerate(far):
        straight, across, later = rest[3 * k : 3 * k + 3]
        total = terms(s | 2)
        across[...] = total[:part].astype(across.dtype)
        relay[k * part : (k + 1) * part, :] = total[part:].astype(relay.dtype)
        total = terms(s)
        straight[...] = total[:part].astype(straight.dtype)
        later[...] = total[part:]


def weight_terms(x, g_parts, members, spread, close):
    count, height, rows = x.shape
    width = g_parts[0].shape[1]
    vmem = pl.BlockSpec(memory_space=pltpu.VMEM)
    height = height // len(spread)
    part = height // 2
    far = len(spread) // 2 - 1
    out = [
        jax.ShapeDtypeStruct((height, width), jnp.float32),
        jax.ShapeDtypeStruct((height, width), jnp.bfloat16),
    ]
    if not close:
        out = [jax.ShapeDtypeStruct((far * part, width), jnp.bfloat16)]
    for _ in range(0 if close else far):
        out += [jax.ShapeDtypeStruct((part, width), jnp.bfloat16)] * 2
        out += [jax.ShapeDtypeStruct((part, width), jnp.float32)]
    return pl.pallas_call(
        functools.partial(weight_kernel, members=members, spread=spread, close=close),
        out_shape=out,
        in_specs=[vmem] * (count + 1),
        out_specs=[vmem] * len(out),
        scratch_shapes=[pltpu.VMEM((count * rows, width), jnp.bfloat16)],
        cost_estimate=pl.CostEstimate(
            flops=x.size * width, bytes_accessed=4 << 20, transcendentals=0
        ),
        compiler_params=pltpu.CompilerParams(vmem_limit_bytes=24 << 20),
        name="weight_terms",
    )(x, *g_parts)


def columns_kernel(x_hbm, _, out_hbm, x, xt, in_sems, out_sems, *, places, height):
    rows, width = x.shape
    step = width // in_sems.shape[0]

    def load(c):
        cols = pl.ds(c * step, step)
        return pltpu.make_async_copy(x_hbm.at[:, cols], x.at[:, cols], in_sems.at[c])

    def store(p):
        (row, line), begin = places[p]
        return pltpu.make_async_copy(
            xt.at[pl.ds(begin, height)], out_hbm.at[row, pl.ds(line, height)], out_sems.at[p]
        )

    chunks = range(in_sems.shape[0])
    for c in chunks:
        load(c).start()
    for c in chunks:
        load(c).wait()
        for begin in range(c * step, (c + 1) * step, 256):
            xt[begin : begin + 256, :] = x[:, begin : begin + 256].T
        for p, (_, begin) in enumerate(places):
            if c * step <= begin < (c + 1) * step:
                store(p).start()
    for p in range(len(places)):
        store(p).wait()


def columns_first(x, early, members, spread, n, dps):
    rows, width = x.shape
    height = width // (n * dps)
    places = [
        ((place, k * height), ((m | s) * dps + i) * height)
        for place, (i, m) in enumerate(members)
        for k, s in enumerate(spread)
    ]
    hbm = pl.BlockSpec(memory_space=pltpu.HBM)
    return pl.pallas_call(
        functools.partial(columns_kernel, places=places, height=height),
        out_shape=jax.ShapeDtypeStruct((len(members), len(spread) * height, rows), x.dtype),
        in_specs=[hbm, pl.BlockSpec(memory_space=pl.ANY)],
        out_specs=hbm,
        scratch_shapes=[
            pltpu.VMEM((rows, width), x.dtype),
            pltpu.VMEM((width, rows), x.dtype),
            pltpu.SemaphoreType.DMA((4,)),
            pltpu.SemaphoreType.DMA((len(places),)),
        ],
        cost_estimate=pl.CostEstimate(
            flops=0, bytes_accessed=4 * rows * width, transcendentals=0
        ),
        compiler_params=pltpu.CompilerParams(vmem_limit_bytes=60 << 20),
        name="columns_first",
    )(x, early)


def after(x, *earlier):
    return lax.optimization_barrier((x, *earlier))[0]


def per_device(layer_input, queries, keys, values, d_out, doc_lengths, block_order):
    n = lax.axis_size("ctx")
    dps = lax.axis_size("dp")
    rows = queries.shape[1]
    head_dim = keys.shape[2]
    width = layer_input.shape[2]
    top = 4
    mid = n // (2 * top)

    def swap(x, k):
        return lax.ppermute(x, "ctx", [(i, i ^ k) for i in range(n)])

    joint = ("dp", "ctx")
    kept = 5 if n >= 8 else n - 1
    spread = [m for m in range(n) if not m & kept]
    members = [(i, m) for i in range(dps) for m in range(n) if not m & ~kept]

    def cross(x, i, m):
        return lax.ppermute(
            x, joint, [(a * n + b, (a ^ i) * n + (b ^ m)) for a in range(dps) for b in range(n)]
        )

    kv = jnp.concatenate([keys[0], values[0]], axis=1)
    tops = [kv] + [swap(kv, 2 * mid * j) for j in range(1, top)]
    base = jnp.stack(tops)

    xt = columns_first(layer_input[0], kv, members, spread, n, dps)
    base = after(base, xt)

    near = [base] + [swap(base, 2 * j) for j in range(1, mid)]
    far = [swap(part, 1) for part in near]
    groups = [[i * n + (m | s) for i, m in members] for s in spread]
    xt = lax.all_to_all(xt, joint, 0, 0, axis_index_groups=groups, tiled=True)

    dq, *parts = attention(
        block_order, doc_lengths, queries[0], d_out[0], near + far, n=n, mid=mid, top=top
    )

    mine, others = parts[:mid], parts[mid:]
    received = [swap(p, 1) for p in reversed(others)][::-1]
    keep = mine[0][0].astype(jnp.float32) + received[0][0].astype(jnp.float32)
    total = mine[0][1:].astype(jnp.float32) + received[0][1:].astype(jnp.float32)
    for j in range(1, mid):
        sent = (mine[j].astype(jnp.float32) + received[j].astype(jnp.float32)).astype(jnp.bfloat16)
        total = total + swap(sent[1:], 2 * j).astype(jnp.float32)
        keep = keep + swap(sent[0], 2 * j).astype(jnp.float32)
    total = total.astype(jnp.bfloat16)
    grad = keep
    for j in range(1, top):
        grad = grad + swap(total[j - 1], 2 * mid * j).astype(jnp.float32)
    grad16 = grad.astype(jnp.bfloat16)

    gathered = {}
    for i, m in members:
        if not m & 1:
            gathered[i, m] = cross(grad16, i, m) if i or m else grad16
    for i, m in members:
        if m & 1:
            gathered[i, m] = swap(gathered[i, m ^ 1], 1)

    terms = functools.partial(weight_terms, xt, [gathered[k] for k in members], members, spread)
    relay, *rest = terms(False)
    keep, close = terms(True)
    height = keep.shape[0]
    part = height // 2
    came = swap(relay, 2).astype(jnp.float32)
    close = swap(close, 2).astype(jnp.float32)
    upper = keep[:part] + close[:part]
    lower = keep[part:] + close[part:]
    for k, s in enumerate(s for s in spread if s and not s & 2):
        straight, across, later = rest[3 * k : 3 * k + 3]
        upper = upper + swap(straight, s).astype(jnp.float32)
        upper = upper + swap(across, s | 2).astype(jnp.float32)
        later = later + came[k * part : (k + 1) * part]
        lower = lower + swap(later.astype(jnp.bfloat16), s).astype(jnp.float32)
    weight = jnp.concatenate([upper, lower], axis=0)
    weight = weight * (1.0 / math.sqrt(dps * rows * n))
    return (
        dq[None],
        grad16[None, :, :head_dim],
        grad16[None, :, head_dim:],
        weight[None],
    )


def solution(mesh):
    placed = (
        P("dp", "ctx", None),
        P("dp", "ctx", None),
        P("dp", "ctx", None),
        P("dp", "ctx", None),
        P("dp", "ctx", None),
        P("dp", None),
        P(),
    )
    return jax.shard_map(
        per_device,
        mesh=mesh,
        in_specs=placed,
        out_specs=(
            P("dp", "ctx", None),
            P("dp", "ctx", None),
            P("dp", "ctx", None),
            P("ctx", "dp", None),
        ),
        check_vma=False,
    )
```

```python
import functools
import math

import jax
import jax.numpy as jnp
from jax import lax
from jax.experimental import pallas as pl
from jax.experimental.pallas import tpu as pltpu
from jax.sharding import PartitionSpec as P

NEG = -1e30
NT = (((1,), (1,)), ((), ()))
TN = (((0,), (0,)), ((), ()))


def attention_kernel(
    order, lengths, q_ref, d_ref, *refs, mid, top, heads, head_dim, half, blocks, window, group
):
    count = 2 * mid
    kv_refs = refs[:count]
    dq_ref = refs[count]
    out_refs = refs[count + 1 : 2 * count + 1]
    kv, kw, acc, inverse = refs[2 * count + 1 :]
    rank = lax.axis_index("ctx")
    rows = 2 * half
    share = top * rows
    for part in range(count):
        kv[part * share : (part + 1) * share, :] = kv_refs[part][...].reshape(share, 2 * head_dim)
    acc[...] = jnp.zeros_like(acc)

    for i in range(blocks):
        rel = jnp.bitwise_xor(rank, i // 2)
        part = (rel & 1) * mid + ((rel >> 1) & (mid - 1))
        inverse[order[i]] = (part * top + (rel >> mid.bit_length())) * rows + (i % 2) * half
    ends = []
    total = 0
    for k in range(lengths.shape[1]):
        total = total + lengths[0, k]
        ends.append(total)
    span = window * half
    scale = 1.0 / math.sqrt(head_dim)
    factor = scale * math.log2(math.e)
    lanes = group * half

    for t in range(2):
        block = order[2 * rank + t]
        first = jnp.clip(block - (window - 1), 0, blocks - window)
        for w in range(window):
            source = pl.multiple_of(inverse[first + w], half)
            kw[w * half : (w + 1) * half, :] = kv[pl.ds(source, half), :]
        k = kw[:, :head_dim]
        v = kw[:, head_dim:]
        tile = 2 * half
        kpos = first * half + lax.broadcasted_iota(jnp.int32, (span, tile), 0)
        qpos = block * half + lax.broadcasted_iota(jnp.int32, (1, tile), 1) % half
        start = jnp.zeros((1, tile), jnp.int32)
        for end in ends:
            start = jnp.where(qpos >= end, end, start)
        hidden = jnp.where((kpos <= qpos) & (kpos >= start), 0.0, NEG)
        hidden = jnp.concatenate([hidden] * (lanes // tile), axis=1)
        dk = jnp.zeros((span, head_dim), jnp.float32)
        dv = jnp.zeros((span, head_dim), jnp.float32)
        trows = slice(t * half, (t + 1) * half)
        for g in range(heads // group):
            cols = [slice(h * head_dim, (h + 1) * head_dim) for h in range(g * group, (g + 1) * group)]
            q = jnp.concatenate([q_ref[trows, c] for c in cols], axis=0)
            d = jnp.concatenate([d_ref[trows, c] for c in cols], axis=0)
            s = lax.dot_general(k, q, NT, preferred_element_type=jnp.float32) * factor
            s = s + hidden
            e = jnp.exp2(s - jnp.max(s, axis=0, keepdims=True))
            inv = 1.0 / jnp.sum(e, axis=0, keepdims=True)
            dp = lax.dot_general(v, d, NT, preferred_element_type=jnp.float32)
            delta = jnp.sum(e * dp, axis=0, keepdims=True) * inv
            p = e * inv
            pb = p.astype(jnp.bfloat16)
            ds = (p * (dp - delta)).astype(jnp.bfloat16)
            dv = dv + jnp.dot(pb, d, preferred_element_type=jnp.float32)
            dk = dk + jnp.dot(ds, q, preferred_element_type=jnp.float32)
            dq = lax.dot_general(k, ds, TN, preferred_element_type=jnp.float32) * scale
            dq = dq.T.astype(jnp.bfloat16)
            for i, c in enumerate(cols):
                dq_ref[trows, c] = dq[i * half : (i + 1) * half, :]
        dk = dk * scale
        for w in range(window):
            target = pl.ds(pl.multiple_of(inverse[first + w], half), half)
            acc[target, :head_dim] += dk[w * half : (w + 1) * half]
            acc[target, head_dim:] += dv[w * half : (w + 1) * half]
    for part in range(count):
        piece = acc[part * share : (part + 1) * share, :]
        out_refs[part][...] = piece.reshape(out_refs[part].shape).astype(out_refs[part].dtype)


def attention(order, lengths, q, d, kv_parts, *, n, mid, top):
    rows, width = q.shape
    head_dim = kv_parts[0].shape[2] // 2
    heads = width // head_dim
    half = rows // 2
    blocks = order.shape[0]
    window = min(blocks, blocks // 4 + 1)
    count = 2 * mid
    part = (top, rows, 2 * head_dim)
    body = functools.partial(
        attention_kernel,
        mid=mid,
        top=top,
        heads=heads,
        head_dim=head_dim,
        half=half,
        blocks=blocks,
        window=window,
        group=min(heads, 8),
    )
    vmem = pl.BlockSpec(memory_space=pltpu.VMEM)
    smem = pl.BlockSpec(memory_space=pltpu.SMEM)
    elements = 2 * heads * half * window * half
    return pl.pallas_call(
        body,
        out_shape=[jax.ShapeDtypeStruct((rows, width), jnp.bfloat16)]
        + [
            jax.ShapeDtypeStruct(part, jnp.float32 if i == 0 else jnp.bfloat16)
            for i in range(count)
        ],
        in_specs=[smem, smem, vmem, vmem] + [vmem] * count,
        out_specs=[vmem] * (count + 1),
        scratch_shapes=[
            pltpu.VMEM((n * rows, 2 * head_dim), jnp.bfloat16),
            pltpu.VMEM((window * half, 2 * head_dim), jnp.bfloat16),
            pltpu.VMEM((n * rows, 2 * head_dim), jnp.float32),
            pltpu.SMEM((blocks,), jnp.int32),
        ],
        cost_estimate=pl.CostEstimate(
            flops=220 * elements * head_dim, bytes_accessed=4 << 20, transcendentals=elements
        ),
        compiler_params=pltpu.CompilerParams(vmem_limit_bytes=40 << 20),
        name="attention_grads",
    )(order, lengths, q, d, *kv_parts)


def weight_kernel(x_ref, *refs, members, spread, close):
    count = len(members)
    g_refs = refs[:count]
    out_refs = refs[count:-1]
    g_all = refs[-1]
    mask = members[-1][1]
    my_dp, my_ctx = lax.axis_index("dp"), lax.axis_index("ctx")
    mine = jnp.int32(0)
    for place, (i, m) in enumerate(members):
        mine = jnp.where((my_dp == i) & ((my_ctx & mask) == m), place, mine)
    rows = g_refs[0].shape[0]
    for rel in range(count):
        place = pl.multiple_of(jnp.bitwise_xor(mine, rel) * rows, rows)
        g_all[pl.ds(place, rows), :] = g_refs[rel][...]
    height = x_ref.shape[1] // len(spread)
    part = height // 2
    me = my_ctx & ~mask
    far = [s for s in spread if s and not s & 2]

    def terms(image):
        begin = jnp.int32(0)
        for place, s in enumerate(spread):
            begin = jnp.where(jnp.bitwise_xor(me, image) == s, place * height, begin)
        begin = pl.multiple_of(begin, height)
        total = jnp.zeros((height, g_all.shape[1]), jnp.float32)
        for src in range(count):
            total = total + jnp.dot(
                x_ref[src, pl.ds(begin, height), :],
                g_all[src * rows : (src + 1) * rows, :],
                preferred_element_type=jnp.float32,
            )
        return total

    if close:
        keep, near = out_refs
        near[...] = terms(2).astype(near.dtype)
        keep[...] = terms(0)
        return
    relay, *rest = out_refs
    for k, s in enumerate(far):
        straight, across, later = rest[3 * k : 3 * k + 3]
        total = terms(s | 2)
        across[...] = total[:part].astype(across.dtype)
        relay[k * part : (k + 1) * part, :] = total[part:].astype(relay.dtype)
        total = terms(s)
        straight[...] = total[:part].astype(straight.dtype)
        later[...] = total[part:]


def weight_terms(x, g_parts, members, spread, close):
    count, height, rows = x.shape
    width = g_parts[0].shape[1]
    vmem = pl.BlockSpec(memory_space=pltpu.VMEM)
    height = height // len(spread)
    part = height // 2
    far = len(spread) // 2 - 1
    out = [
        jax.ShapeDtypeStruct((height, width), jnp.float32),
        jax.ShapeDtypeStruct((height, width), jnp.bfloat16),
    ]
    if not close:
        out = [jax.ShapeDtypeStruct((far * part, width), jnp.bfloat16)]
    for _ in range(0 if close else far):
        out += [jax.ShapeDtypeStruct((part, width), jnp.bfloat16)] * 2
        out += [jax.ShapeDtypeStruct((part, width), jnp.float32)]
    return pl.pallas_call(
        functools.partial(weight_kernel, members=members, spread=spread, close=close),
        out_shape=out,
        in_specs=[vmem] * (count + 1),
        out_specs=[vmem] * len(out),
        scratch_shapes=[pltpu.VMEM((count * rows, width), jnp.bfloat16)],
        cost_estimate=pl.CostEstimate(
            flops=x.size * width, bytes_accessed=4 << 20, transcendentals=0
        ),
        compiler_params=pltpu.CompilerParams(vmem_limit_bytes=24 << 20),
        name="weight_terms",
    )(x, *g_parts)


def columns_kernel(x_hbm, _, out_hbm, x, xt, in_sems, out_sems, *, places, height):
    rows, width = x.shape
    step = width // in_sems.shape[0]

    def load(c):
        cols = pl.ds(c * step, step)
        return pltpu.make_async_copy(x_hbm.at[:, cols], x.at[:, cols], in_sems.at[c])

    def store(p):
        (row, line), begin = places[p]
        return pltpu.make_async_copy(
            xt.at[pl.ds(begin, height)], out_hbm.at[row, pl.ds(line, height)], out_sems.at[p]
        )

    chunks = range(in_sems.shape[0])
    for c in chunks:
        load(c).start()
    for c in chunks:
        load(c).wait()
        for begin in range(c * step, (c + 1) * step, 256):
            xt[begin : begin + 256, :] = x[:, begin : begin + 256].T
        for p, (_, begin) in enumerate(places):
            if c * step <= begin < (c + 1) * step:
                store(p).start()
    for p in range(len(places)):
        store(p).wait()


def columns_first(x, early, members, spread, n, dps):
    rows, width = x.shape
    height = width // (n * dps)
    places = [
        ((place, k * height), ((m | s) * dps + i) * height)
        for place, (i, m) in enumerate(members)
        for k, s in enumerate(spread)
    ]
    hbm = pl.BlockSpec(memory_space=pltpu.HBM)
    return pl.pallas_call(
        functools.partial(columns_kernel, places=places, height=height),
        out_shape=jax.ShapeDtypeStruct((len(members), len(spread) * height, rows), x.dtype),
        in_specs=[hbm, pl.BlockSpec(memory_space=pl.ANY)],
        out_specs=hbm,
        scratch_shapes=[
            pltpu.VMEM((rows, width), x.dtype),
            pltpu.VMEM((width, rows), x.dtype),
            pltpu.SemaphoreType.DMA((4,)),
            pltpu.SemaphoreType.DMA((len(places),)),
        ],
        cost_estimate=pl.CostEstimate(
            flops=0, bytes_accessed=4 * rows * width, transcendentals=0
        ),
        compiler_params=pltpu.CompilerParams(vmem_limit_bytes=60 << 20),
        name="columns_first",
    )(x, early)


def after(x, *earlier):
    return lax.optimization_barrier((x, *earlier))[0]


def per_device(layer_input, queries, keys, values, d_out, doc_lengths, block_order):
    n = lax.axis_size("ctx")
    dps = lax.axis_size("dp")
    rows = queries.shape[1]
    head_dim = keys.shape[2]
    width = layer_input.shape[2]
    top = 4
    mid = n // (2 * top)

    def swap(x, k):
        return lax.ppermute(x, "ctx", [(i, i ^ k) for i in range(n)])

    joint = ("dp", "ctx")
    kept = 5 if n >= 8 else n - 1
    spread = [m for m in range(n) if not m & kept]
    members = [(i, m) for i in range(dps) for m in range(n) if not m & ~kept]

    def cross(x, i, m):
        return lax.ppermute(
            x, joint, [(a * n + b, (a ^ i) * n + (b ^ m)) for a in range(dps) for b in range(n)]
        )

    kv = jnp.concatenate([keys[0], values[0]], axis=1)
    tops = [kv] + [swap(kv, 2 * mid * j) for j in range(1, top)]
    base = jnp.stack(tops)

    xt = columns_first(layer_input[0], kv, members, spread, n, dps)
    base = after(base, xt)

    near = [base] + [swap(base, 2 * j) for j in range(1, mid)]
    far = [swap(part, 1) for part in near]
    groups = [[i * n + (m | s) for i, m in members] for s in spread]
    xt = lax.all_to_all(xt, joint, 0, 0, axis_index_groups=groups, tiled=True)

    dq, *parts = attention(
        block_order, doc_lengths, queries[0], d_out[0], near + far, n=n, mid=mid, top=top
    )

    mine, others = parts[:mid], parts[mid:]
    received = [swap(p, 1) for p in reversed(others)][::-1]
    keep = mine[0][0].astype(jnp.float32) + received[0][0].astype(jnp.float32)
    total = mine[0][1:].astype(jnp.float32) + received[0][1:].astype(jnp.float32)
    for j in range(1, mid):
        sent = (mine[j].astype(jnp.float32) + received[j].astype(jnp.float32)).astype(jnp.bfloat16)
        total = total + swap(sent[1:], 2 * j).astype(jnp.float32)
        keep = keep + swap(sent[0], 2 * j).astype(jnp.float32)
    total = total.astype(jnp.bfloat16)
    grad = keep
    for j in range(1, top):
        grad = grad + swap(total[j - 1], 2 * mid * j).astype(jnp.float32)
    grad16 = grad.astype(jnp.bfloat16)

    gathered = {}
    for i, m in members:
        if not m & 1:
            gathered[i, m] = cross(grad16, i, m) if i or m else grad16
    for i, m in members:
        if m & 1:
            gathered[i, m] = swap(gathered[i, m ^ 1], 1)

    terms = functools.partial(weight_terms, xt, [gathered[k] for k in members], members, spread)
    relay, *rest = terms(False)
    keep, close = terms(True)
    height = keep.shape[0]
    part = height // 2
    came = swap(relay, 2).astype(jnp.float32)
    close = swap(close, 2).astype(jnp.float32)
    upper = keep[:part] + close[:part]
    lower = keep[part:] + close[part:]
    for k, s in enumerate(s for s in spread if s and not s & 2):
        straight, across, later = rest[3 * k : 3 * k + 3]
        upper = upper + swap(straight, s).astype(jnp.float32)
        upper = upper + swap(across, s | 2).astype(jnp.float32)
        later = later + came[k * part : (k + 1) * part]
        lower = lower + swap(later.astype(jnp.bfloat16), s).astype(jnp.float32)
    weight = jnp.concatenate([upper, lower], axis=0)
    weight = weight * (1.0 / math.sqrt(dps * rows * n))
    return (
        dq[None],
        grad16[None, :, :head_dim],
        grad16[None, :, head_dim:],
        weight[None],
    )


def solution(mesh):
    placed = (
        P("dp", "ctx", None),
        P("dp", "ctx", None),
        P("dp", "ctx", None),
        P("dp", "ctx", None),
        P("dp", "ctx", None),
        P("dp", None),
        P(),
    )
    return jax.shard_map(
        per_device,
        mesh=mesh,
        in_specs=placed,
        out_specs=(
            P("dp", "ctx", None),
            P("dp", "ctx", None),
            P("dp", "ctx", None),
            P("ctx", "dp", None),
        ),
        check_vma=False,
    )
```

```python
import functools
import math

import jax
import jax.numpy as jnp
from jax import lax
from jax.experimental import pallas as pl
from jax.experimental.pallas import tpu as pltpu
from jax.sharding import PartitionSpec as P

NEG = -1e30
NT = (((1,), (1,)), ((), ()))
TN = (((0,), (0,)), ((), ()))


def attention_kernel(
    order, lengths, q_ref, d_ref, *refs, mid, top, heads, head_dim, half, blocks, window, group
):
    count = 2 * mid
    kv_refs = refs[:count]
    dq_ref = refs[count]
    out_refs = refs[count + 1 : 2 * count + 1]
    kv, kw, acc, inverse = refs[2 * count + 1 :]
    rank = lax.axis_index("ctx")
    rows = 2 * half
    share = top * rows
    for part in range(count):
        kv[part * share : (part + 1) * share, :] = kv_refs[part][...].reshape(share, 2 * head_dim)
    acc[...] = jnp.zeros_like(acc)

    for i in range(blocks):
        rel = jnp.bitwise_xor(rank, i // 2)
        part = (rel & 1) * mid + ((rel >> 1) & (mid - 1))
        inverse[order[i]] = (part * top + (rel >> mid.bit_length())) * rows + (i % 2) * half
    ends = []
    total = 0
    for k in range(lengths.shape[1]):
        total = total + lengths[0, k]
        ends.append(total)
    span = window * half
    scale = 1.0 / math.sqrt(head_dim)
    factor = scale * math.log2(math.e)
    lanes = group * half

    for t in range(2):
        block = order[2 * rank + t]
        first = jnp.clip(block - (window - 1), 0, blocks - window)
        for w in range(window):
            source = pl.multiple_of(inverse[first + w], half)
            kw[w * half : (w + 1) * half, :] = kv[pl.ds(source, half), :]
        k = kw[:, :head_dim]
        v = kw[:, head_dim:]
        tile = 2 * half
        kpos = first * half + lax.broadcasted_iota(jnp.int32, (span, tile), 0)
        qpos = block * half + lax.broadcasted_iota(jnp.int32, (1, tile), 1) % half
        start = jnp.zeros((1, tile), jnp.int32)
        for end in ends:
            start = jnp.where(qpos >= end, end, start)
        hidden = jnp.where((kpos <= qpos) & (kpos >= start), 0.0, NEG)
        hidden = jnp.concatenate([hidden] * (lanes // tile), axis=1)
        dk = jnp.zeros((span, head_dim), jnp.float32)
        dv = jnp.zeros((span, head_dim), jnp.float32)
        trows = slice(t * half, (t + 1) * half)
        for g in range(heads // group):
            cols = [slice(h * head_dim, (h + 1) * head_dim) for h in range(g * group, (g + 1) * group)]
            q = jnp.concatenate([q_ref[trows, c] for c in cols], axis=0)
            d = jnp.concatenate([d_ref[trows, c] for c in cols], axis=0)
            s = lax.dot_general(k, q, NT, preferred_element_type=jnp.float32) * factor
            s = s + hidden
            e = jnp.exp2(s - jnp.max(s, axis=0, keepdims=True))
            inv = 1.0 / jnp.sum(e, axis=0, keepdims=True)
            dp = lax.dot_general(v, d, NT, preferred_element_type=jnp.float32)
            delta = jnp.sum(e * dp, axis=0, keepdims=True) * inv
            p = e * inv
            pb = p.astype(jnp.bfloat16)
            ds = (p * (dp - delta)).astype(jnp.bfloat16)
            dv = dv + jnp.dot(pb, d, preferred_element_type=jnp.float32)
            dk = dk + jnp.dot(ds, q, preferred_element_type=jnp.float32)
            dq = lax.dot_general(k, ds, TN, preferred_element_type=jnp.float32) * scale
            dq = dq.T.astype(jnp.bfloat16)
            for i, c in enumerate(cols):
                dq_ref[trows, c] = dq[i * half : (i + 1) * half, :]
        dk = dk * scale
        for w in range(window):
            target = pl.ds(pl.multiple_of(inverse[first + w], half), half)
            acc[target, :head_dim] += dk[w * half : (w + 1) * half]
            acc[target, head_dim:] += dv[w * half : (w + 1) * half]
    for part in range(count):
        piece = acc[part * share : (part + 1) * share, :]
        out_refs[part][...] = piece.reshape(out_refs[part].shape).astype(out_refs[part].dtype)


def attention(order, lengths, q, d, kv_parts, *, n, mid, top):
    rows, width = q.shape
    head_dim = kv_parts[0].shape[2] // 2
    heads = width // head_dim
    half = rows // 2
    blocks = order.shape[0]
    window = min(blocks, blocks // 4 + 1)
    count = 2 * mid
    part = (top, rows, 2 * head_dim)
    body = functools.partial(
        attention_kernel,
        mid=mid,
        top=top,
        heads=heads,
        head_dim=head_dim,
        half=half,
        blocks=blocks,
        window=window,
        group=min(heads, 8),
    )
    vmem = pl.BlockSpec(memory_space=pltpu.VMEM)
    smem = pl.BlockSpec(memory_space=pltpu.SMEM)
    elements = 2 * heads * half * window * half
    return pl.pallas_call(
        body,
        out_shape=[jax.ShapeDtypeStruct((rows, width), jnp.bfloat16)]
        + [
            jax.ShapeDtypeStruct(part, jnp.float32 if i == 0 else jnp.bfloat16)
            for i in range(count)
        ],
        in_specs=[smem, smem, vmem, vmem] + [vmem] * count,
        out_specs=[vmem] * (count + 1),
        scratch_shapes=[
            pltpu.VMEM((n * rows, 2 * head_dim), jnp.bfloat16),
            pltpu.VMEM((window * half, 2 * head_dim), jnp.bfloat16),
            pltpu.VMEM((n * rows, 2 * head_dim), jnp.float32),
            pltpu.SMEM((blocks,), jnp.int32),
        ],
        cost_estimate=pl.CostEstimate(
            flops=220 * elements * head_dim, bytes_accessed=4 << 20, transcendentals=elements
        ),
        compiler_params=pltpu.CompilerParams(vmem_limit_bytes=40 << 20),
        name="attention_grads",
    )(order, lengths, q, d, *kv_parts)


def weight_kernel(x_ref, *refs, members, spread, close):
    count = len(members)
    g_refs = refs[:count]
    out_refs = refs[count:-1]
    g_all = refs[-1]
    mask = members[-1][1]
    my_dp, my_ctx = lax.axis_index("dp"), lax.axis_index("ctx")
    mine = jnp.int32(0)
    for place, (i, m) in enumerate(members):
        mine = jnp.where((my_dp == i) & ((my_ctx & mask) == m), place, mine)
    rows = g_refs[0].shape[0]
    for rel in range(count):
        place = pl.multiple_of(jnp.bitwise_xor(mine, rel) * rows, rows)
        g_all[pl.ds(place, rows), :] = g_refs[rel][...]
    height = x_ref.shape[1] // len(spread)
    part = height // 2
    me = my_ctx & ~mask
    far = [s for s in spread if s and not s & 2]

    def terms(image):
        begin = jnp.int32(0)
        for place, s in enumerate(spread):
            begin = jnp.where(jnp.bitwise_xor(me, image) == s, place * height, begin)
        begin = pl.multiple_of(begin, height)
        total = jnp.zeros((height, g_all.shape[1]), jnp.float32)
        for src in range(count):
            total = total + jnp.dot(
                x_ref[src, pl.ds(begin, height), :],
                g_all[src * rows : (src + 1) * rows, :],
                preferred_element_type=jnp.float32,
            )
        return total

    if close:
        keep, near = out_refs
        near[...] = terms(2).astype(near.dtype)
        keep[...] = terms(0)
        return
    relay, *rest = out_refs
    for k, s in enumerate(far):
        straight, across, later = rest[3 * k : 3 * k + 3]
        total = terms(s | 2)
        across[...] = total[:part].astype(across.dtype)
        relay[k * part : (k + 1) * part, :] = total[part:].astype(relay.dtype)
        total = terms(s)
        straight[...] = total[:part].astype(straight.dtype)
        later[...] = total[part:]


def weight_terms(x, g_parts, members, spread, close):
    count, height, rows = x.shape
    width = g_parts[0].shape[1]
    vmem = pl.BlockSpec(memory_space=pltpu.VMEM)
    height = height // len(spread)
    part = height // 2
    far = len(spread) // 2 - 1
    out = [
        jax.ShapeDtypeStruct((height, width), jnp.float32),
        jax.ShapeDtypeStruct((height, width), jnp.bfloat16),
    ]
    if not close:
        out = [jax.ShapeDtypeStruct((far * part, width), jnp.bfloat16)]
    for _ in range(0 if close else far):
        out += [jax.ShapeDtypeStruct((part, width), jnp.bfloat16)] * 2
        out += [jax.ShapeDtypeStruct((part, width), jnp.float32)]
    return pl.pallas_call(
        functools.partial(weight_kernel, members=members, spread=spread, close=close),
        out_shape=out,
        in_specs=[vmem] * (count + 1),
        out_specs=[vmem] * len(out),
        scratch_shapes=[pltpu.VMEM((count * rows, width), jnp.bfloat16)],
        cost_estimate=pl.CostEstimate(
            flops=x.size * width, bytes_accessed=4 << 20, transcendentals=0
        ),
        compiler_params=pltpu.CompilerParams(vmem_limit_bytes=24 << 20),
        name="weight_terms",
    )(x, *g_parts)


def columns_kernel(x_hbm, _, out_hbm, x, xt, in_sems, out_sems, *, places, height):
    rows, width = x.shape
    step = width // in_sems.shape[0]

    def load(c):
        cols = pl.ds(c * step, step)
        return pltpu.make_async_copy(x_hbm.at[:, cols], x.at[:, cols], in_sems.at[c])

    def store(p):
        (row, line), begin = places[p]
        return pltpu.make_async_copy(
            xt.at[pl.ds(begin, height)], out_hbm.at[row, pl.ds(line, height)], out_sems.at[p]
        )

    chunks = range(in_sems.shape[0])
    for c in chunks:
        load(c).start()
    for c in chunks:
        load(c).wait()
        for begin in range(c * step, (c + 1) * step, 256):
            xt[begin : begin + 256, :] = x[:, begin : begin + 256].T
        for p, (_, begin) in enumerate(places):
            if c * step <= begin < (c + 1) * step:
                store(p).start()
    for p in range(len(places)):
        store(p).wait()


def columns_first(x, early, members, spread, n, dps):
    rows, width = x.shape
    height = width // (n * dps)
    places = [
        ((place, k * height), ((m | s) * dps + i) * height)
        for place, (i, m) in enumerate(members)
        for k, s in enumerate(spread)
    ]
    hbm = pl.BlockSpec(memory_space=pltpu.HBM)
    return pl.pallas_call(
        functools.partial(columns_kernel, places=places, height=height),
        out_shape=jax.ShapeDtypeStruct((len(members), len(spread) * height, rows), x.dtype),
        in_specs=[hbm, pl.BlockSpec(memory_space=pl.ANY)],
        out_specs=hbm,
        scratch_shapes=[
            pltpu.VMEM((rows, width), x.dtype),
            pltpu.VMEM((width, rows), x.dtype),
            pltpu.SemaphoreType.DMA((4,)),
            pltpu.SemaphoreType.DMA((len(places),)),
        ],
        cost_estimate=pl.CostEstimate(
            flops=0, bytes_accessed=4 * rows * width, transcendentals=0
        ),
        compiler_params=pltpu.CompilerParams(vmem_limit_bytes=60 << 20),
        name="columns_first",
    )(x, early)


def after(x, *earlier):
    return lax.optimization_barrier((x, *earlier))[0]


def per_device(layer_input, queries, keys, values, d_out, doc_lengths, block_order):
    n = lax.axis_size("ctx")
    dps = lax.axis_size("dp")
    rows = queries.shape[1]
    head_dim = keys.shape[2]
    width = layer_input.shape[2]
    top = 4
    mid = n // (2 * top)

    def swap(x, k):
        return lax.ppermute(x, "ctx", [(i, i ^ k) for i in range(n)])

    joint = ("dp", "ctx")
    kept = 5 if n >= 8 else n - 1
    spread = [m for m in range(n) if not m & kept]
    members = [(i, m) for i in range(dps) for m in range(n) if not m & ~kept]

    def cross(x, i, m):
        return lax.ppermute(
            x, joint, [(a * n + b, (a ^ i) * n + (b ^ m)) for a in range(dps) for b in range(n)]
        )

    kv = jnp.concatenate([keys[0], values[0]], axis=1)
    tops = {j: swap(kv, 2 * mid * j) for j in (1, 3, 2)}
    tops = [kv] + [tops[j] for j in range(1, top)]
    base = jnp.stack(tops)

    xt = columns_first(layer_input[0], kv, members, spread, n, dps)
    base = after(base, xt)

    near = [base] + [swap(base, 2 * j) for j in range(1, mid)]
    far = [swap(part, 1) for part in near]
    groups = [[i * n + (m | s) for i, m in members] for s in spread]
    xt = lax.all_to_all(xt, joint, 0, 0, axis_index_groups=groups, tiled=True)

    dq, *parts = attention(
        block_order, doc_lengths, queries[0], d_out[0], near + far, n=n, mid=mid, top=top
    )

    mine, others = parts[:mid], parts[mid:]
    received = [swap(p, 1) for p in reversed(others)][::-1]
    keep = mine[0][0].astype(jnp.float32) + received[0][0].astype(jnp.float32)
    total = mine[0][1:].astype(jnp.float32) + received[0][1:].astype(jnp.float32)
    for j in range(1, mid):
        sent = (mine[j].astype(jnp.float32) + received[j].astype(jnp.float32)).astype(jnp.bfloat16)
        total = total + swap(sent[1:], 2 * j).astype(jnp.float32)
        keep = keep + swap(sent[0], 2 * j).astype(jnp.float32)
    total = total.astype(jnp.bfloat16)
    grad = keep
    for j in range(1, top):
        grad = grad + swap(total[j - 1], 2 * mid * j).astype(jnp.float32)
    grad16 = grad.astype(jnp.bfloat16)

    gathered = {}
    for i, m in members:
        if not m & 1:
            gathered[i, m] = cross(grad16, i, m) if i or m else grad16
    for i, m in members:
        if m & 1:
            gathered[i, m] = swap(gathered[i, m ^ 1], 1)

    terms = functools.partial(weight_terms, xt, [gathered[k] for k in members], members, spread)
    relay, *rest = terms(False)
    keep, close = terms(True)
    height = keep.shape[0]
    part = height // 2
    came = swap(relay, 2).astype(jnp.float32)
    close = swap(close, 2).astype(jnp.float32)
    upper = keep[:part] + close[:part]
    lower = keep[part:] + close[part:]
    for k, s in enumerate(s for s in spread if s and not s & 2):
        straight, across, later = rest[3 * k : 3 * k + 3]
        upper = upper + swap(straight, s).astype(jnp.float32)
        upper = upper + swap(across, s | 2).astype(jnp.float32)
        later = later + came[k * part : (k + 1) * part]
        lower = lower + swap(later.astype(jnp.bfloat16), s).astype(jnp.float32)
    weight = jnp.concatenate([upper, lower], axis=0)
    weight = weight * (1.0 / math.sqrt(dps * rows * n))
    return (
        dq[None],
        grad16[None, :, :head_dim],
        grad16[None, :, head_dim:],
        weight[None],
    )


def solution(mesh):
    placed = (
        P("dp", "ctx", None),
        P("dp", "ctx", None),
        P("dp", "ctx", None),
        P("dp", "ctx", None),
        P("dp", "ctx", None),
        P("dp", None),
        P(),
    )
    return jax.shard_map(
        per_device,
        mesh=mesh,
        in_specs=placed,
        out_specs=(
            P("dp", "ctx", None),
            P("dp", "ctx", None),
            P("dp", "ctx", None),
            P("ctx", "dp", None),
        ),
        check_vma=False,
    )
```
